128 devices in a mesh: space: 8 (over y_hi, x), chan: 16 (over z, y_lo, core).
Axes of the slice: x: 4, y: 4 (y_hi: 2, y_lo: 2; y = y_hi * 2 + y_lo), z: 4, core: 2. Of those that a mesh axis runs over, the one named last changes fastest.
Arguments:
- layer_input: bfloat16 [8, 16, 256, 128], P('space', None, 'chan'), may hold values from -6 to 6
- pre_act: bfloat16 [8, 16, 256, 128], P('space', None, 'chan'), may hold values from -8 to 8
- out_grad: bfloat16 [8, 16, 256, 128], P('space', None, 'chan'), may hold values from -6 to 6
- weight_one: bfloat16 [27, 256, 256], P(None, 'chan'), may hold values from -0.078125 to 0.078125
- weight_two: bfloat16 [27, 256, 256], P(None, 'chan'), may hold values from -0.078125 to 0.078125
Outputs:
- input_grad: bfloat16 [8, 16, 256, 128], P('space', None, 'chan')
- grad_one: float32 [27, 256, 256], P(None, 'chan', 'space')
- grad_two: float32 [27, 256, 256], P(None, 'chan', 'space')
The draws below stay inside these ranges and needn't reach their ends.
All inputs are finite; a program needn't handle non-finite values.
Results may differ from the reference program's by a relative error of at most 0.0049.
Values may be sent and summed in bfloat16 or wider, within the bound.
A program may use at most 64 MiB of HBM per device.

```python
import jax
import jax.numpy as jnp
from jax import lax

C = 256
NY = 128
NZ = 16
NX = 8


def levels(key, extent, split, low, top_value):
    def one(dim, parts):
        heights = jax.random.uniform(jax.random.fold_in(jax.random.fold_in(key, 6), dim), (parts,), jnp.float32, low / len(split), top_value / len(split))
        return jnp.repeat(jnp.exp(heights), extent[dim] // parts).reshape((-1,) + (1,) * (len(extent) - dim - 1))

    gain = one(*split[0])
    for cut in split[1:]:
        gain = gain * one(*cut)
    return gain


def noise(own_key, extent, deviation, bound, cuts=(), kind=jnp.bfloat16):
    gain = levels(own_key, extent, cuts, -0.22, 0.18) if cuts else 1.0
    array = jax.random.normal(own_key, extent, jnp.float32) * deviation * gain
    return jnp.minimum(jnp.maximum(array, -bound), bound).astype(kind)


def setup_inputs(seed: int = 0) -> dict:
    arg_keys = jax.random.split(jax.random.key(seed), 6)
    layer_input = noise(arg_keys[0], (NX, NZ, C, NY), 1.0, 6.0, ((0, 8), (2, 16)))
    pre_act = noise(arg_keys[1], (NX, NZ, C, NY), 1.5, 8.0, ((0, 8), (2, 16)))
    out_grad = noise(arg_keys[2], (NX, NZ, C, NY), 1.0, 6.0, ((0, 8), (2, 16)))
    weight_one = noise(arg_keys[3], (27, C, C), (27 * C) ** -0.5, 0.078125, ((1, 16),))
    weight_two = noise(arg_keys[4], (27, C, C), (27 * C) ** -0.5, 0.078125, ((1, 16),))
    return {"layer_input": layer_input, "pre_act": pre_act, "out_grad": out_grad, "weight_one": weight_one, "weight_two": weight_two}


def silu_slope(value):
    sig = jax.nn.sigmoid(value)
    return sig * (1.0 + value * (1.0 - sig))


def conv_grads(inp, grad_out, weight):
    in_pad = jnp.pad(inp, ((1, 1), (1, 1), (0, 0), (1, 1)))
    grad_pad = jnp.pad(grad_out, ((1, 1), (1, 1), (0, 0), (1, 1)))
    weight_grads = []
    result = jnp.zeros((NX, NZ, C, NY), jnp.float32)
    index = 0
    for shift_x in range(-1, 2):
        for shift_y in range(-1, 2):
            for shift_z in range(-1, 2):
                window = in_pad[1 + shift_x:1 + shift_x + NX, 1 + shift_z:1 + shift_z + NZ, :, 1 + shift_y:1 + shift_y + NY]
                weight_grads.append(lax.dot_general(window, grad_out, (((0, 1, 3), (0, 1, 3)), ((), ())), preferred_element_type=jnp.float32))
                back = grad_pad[1 - shift_x:1 - shift_x + NX, 1 - shift_z:1 - shift_z + NZ, :, 1 - shift_y:1 - shift_y + NY]
                result = result + jnp.einsum("xzoy,io->xziy", back, weight[index], preferred_element_type=jnp.float32)
                index += 1
    return result, jnp.stack(weight_grads)


def reference(layer_input, pre_act, out_grad, weight_one, weight_two):
    scale = float(NX * NY * NZ) ** -0.5
    pre_float = pre_act.astype(jnp.float32)
    hidden = jax.nn.silu(pre_float).astype(jnp.bfloat16)
    hidden_grad, grad_two = conv_grads(hidden, out_grad, weight_two)
    pre_grad = (hidden_grad * silu_slope(pre_float)).astype(jnp.bfloat16)
    input_grad, grad_one = conv_grads(layer_input, pre_grad, weight_one)
    return input_grad.astype(jnp.bfloat16), grad_one * scale, grad_two * scale
```

```python
import functools

import jax
import jax.numpy as jnp
from jax import lax
from jax.experimental import pallas as pl
from jax.experimental.pallas import tpu as pltpu
from jax.sharding import PartitionSpec as P

MESH = pl.DeviceIdType.MESH
OFFSETS = (-1, 0, 1)
CHIPS = ((2, 2), (2, 0), (1, 2), (3, 2), (1, 0), (3, 0), (0, 2))


def tap(a, b, c):
    return 9 * (a + 1) + 3 * (b + 1) + (c + 1)


def moved(value, step):
    if step == 0:
        return value
    width = value.shape[1]
    lane = lax.broadcasted_iota(jnp.int32, value.shape, 1)
    inside = lane < width - step if step > 0 else lane >= -step
    return jnp.where(inside, pltpu.roll(value, (-step) % width, 1), 0.0)


def kernel(
    dims,
    layer_hbm, pre_hbm, cot_hbm, w1_hbm, w2_hbm,
    out_ref, one_ref, two_ref,
    layer, pre, cot, w1, w2, hid, slope,
    got_cot, got_pre, cols_one, cols_two, prod, center,
    part, send_part, recv_part, send_q, recv_q,
    load_sem, gs, gr, fs, fr, hs, hr, qs, qr, ws, wr,
):
    ns, nz, own, ny, scale = dims
    groups = got_cot.shape[0] // own
    rows = own * nz
    wide = part.shape[0] // ns
    s = lax.axis_index("space")
    c = lax.axis_index("chan")
    zc, wc = lax.div(c, 4), lax.rem(c, 4)
    levels = groups // 4

    def chip(dz, dw):
        return lax.rem(zc + dz, levels) * 4 + (wc ^ dw)

    sibling = (s, c ^ 1)
    mine = pl.ds(pl.multiple_of(c * own, own), own)

    barrier = pltpu.get_barrier_semaphore()
    partners = [(s, chip(*d)) for d in CHIPS] + [(lax.rem(s + d, ns), c) for d in range(1, ns)] + [sibling]
    for p in partners:
        pl.semaphore_signal(barrier, inc=1, device_id=p, device_id_type=MESH)

    loads = [
        pltpu.make_async_copy(src, dst, load_sem.at[k])
        for k, (src, dst) in enumerate(
            ((cot_hbm.at[0], cot), (pre_hbm.at[0], pre), (layer_hbm.at[0], layer.at[1]), (w2_hbm, w2), (w1_hbm, w1))
        )
    ]
    for copy in loads:
        copy.start()

    loads[0].wait()
    for z in range(nz):
        got_cot[mine, z * ny:(z + 1) * ny] = cot[z]
    loads[1].wait()
    value = pre[...].astype(jnp.float32).reshape(rows, ny)
    sig = jax.nn.sigmoid(value)
    hid[1] = (value * sig).astype(jnp.bfloat16).reshape(nz, own, ny)
    slope[...] = sig * (1.0 + value * (1.0 - sig))
    loads[2].wait()

    def fill(cols, field, a):
        plane = field[a + 1].astype(jnp.float32).reshape(rows, ny)
        for b in OFFSETS:
            side = moved(plane, b).astype(jnp.bfloat16)
            for e in OFFSETS:
                k = tap(a, b, e)
                for z in range(nz):
                    if 0 <= z + e < nz:
                        piece = side[(z + e) * own:(z + e + 1) * own]
                    else:
                        piece = jnp.zeros((own, ny), jnp.bfloat16)
                    cols[k * own:(k + 1) * own, z * ny:(z + 1) * ny] = piece

    fill(cols_two, hid, 0)
    fill(cols_one, layer, 0)

    pl.semaphore_wait(barrier, len(partners))

    def start_gather(buf, row):
        home = pltpu.make_async_remote_copy(
            buf.at[mine], buf.at[mine], fs.at[row, 7], fr.at[row, 7], device_id=sibling, device_id_type=MESH
        )
        sends = []
        for k, d in enumerate(CHIPS):
            copy = pltpu.make_async_remote_copy(
                buf.at[mine], buf.at[mine], gs.at[row, k], gr.at[row, k], device_id=(s, chip(*d)), device_id_type=MESH
            )
            copy.start()
            sends.append(copy)
        home.start()
        return home, sends

    def forward_gather(buf, row, home, sends):
        passed = []
        for k in reversed(range(len(CHIPS))):
            dz, dw = CHIPS[k]
            sends[k].wait_recv()
            origin = pl.ds(pl.multiple_of(chip(levels - dz, dw) * own, own), own)
            copy = pltpu.make_async_remote_copy(
                buf.at[origin], buf.at[origin], fs.at[row, k], fr.at[row, k], device_id=sibling, device_id_type=MESH
            )
            copy.start()
            passed.append(copy)
        for copy in [home] + passed:
            copy.wait_recv()
        return [home] + passed + sends

    def halo(src, dst, sem, step, there):
        return pltpu.make_async_remote_copy(
            src, dst, hs.at[sem], hr.at[sem], device_id=(there, c), device_id_type=MESH
        )

    up, down = lax.rem(s + 1, ns), lax.rem(s + ns - 1, ns)

    halo_copies = [
        (halo(hid.at[1], hid.at[0], 0, 1, up), halo(hid.at[1], hid.at[2], 1, -1, down)),
        (halo(layer.at[1], layer.at[0], 2, 1, up), halo(layer.at[1], layer.at[2], 3, -1, down)),
    ]

    def start_pair(pair):
        @pl.when(s < ns - 1)
        def _():
            pair[0].start()

        @pl.when(s > 0)
        def _():
            pair[1].start()

    def finish_pair(pair, low, high):
        @pl.when(s > 0)
        def _():
            pair[0].wait_recv()

        @pl.when(s == 0)
        def _():
            low[...] = jnp.zeros(low.shape, low.dtype)

        @pl.when(s < ns - 1)
        def _():
            pair[1].wait_recv()

        @pl.when(s == ns - 1)
        def _():
            high[...] = jnp.zeros(high.shape, high.dtype)

    def sent_pair(pair):
        @pl.when(s < ns - 1)
        def _():
            pair[0].wait_send()

        @pl.when(s > 0)
        def _():
            pair[1].wait_send()

    def plane_sum(weight, got, a):
        lo = tap(a, -1, -1) * own
        left = weight[9 * (a + 1):9 * (a + 2)].reshape(9 * own, groups * own)
        prod[lo:lo + 9 * own, :] = jnp.dot(left, got[...], preferred_element_type=jnp.float32)
        result = []
        for z in range(nz):
            total = None
            for b in OFFSETS:
                column = None
                for e in OFFSETS:
                    if 0 <= z - e < nz:
                        k = tap(a, b, e)
                        term = prod[k * own:(k + 1) * own, (z - e) * ny:(z - e + 1) * ny]
                        column = term if column is None else column + term
                column = moved(column, -b)
                total = column if total is None else total + column
            result.append(total)
        return result

    def q_pair(row):
        def copy(slot, there):
            return pltpu.make_async_remote_copy(
                send_q.at[row, slot], recv_q.at[row, slot], qs.at[row, slot], qr.at[row, slot],
                device_id=(there, c), device_id_type=MESH,
            )

        return copy(0, up), copy(1, down)

    def input_side(weight, got, row):
        pair = q_pair(row)
        for slot, a in ((0, 1), (1, -1)):
            for z, value in enumerate(plane_sum(weight, got, a)):
                send_q[row, slot, z] = value.astype(jnp.bfloat16)
        start_pair(pair)
        for z, value in enumerate(plane_sum(weight, got, 0)):
            center[z * own:(z + 1) * own, :] = value
        return pair

    def input_total(pair, row):
        finish_pair(pair, recv_q.at[row, 0], recv_q.at[row, 1])
        low = recv_q[row, 0].astype(jnp.float32).reshape(rows, ny)
        high = recv_q[row, 1].astype(jnp.float32).reshape(rows, ny)
        return center[...] + low + high

    def weight_side(cols, got, row):
        part[...] = lax.dot_general(
            got[...], cols[...], (((1,), (1,)), ((), ())), preferred_element_type=jnp.float32
        )
        send_part[row] = part[...].astype(jnp.bfloat16)
        copies = []
        for d in range(1, ns):
            there = lax.rem(s + d, ns)
            block = pl.ds(pl.multiple_of(there * wide, wide), wide)
            copy = pltpu.make_async_remote_copy(
                send_part.at[row, block], recv_part.at[row, d - 1], ws.at[row, d - 1], wr.at[row, d - 1],
                device_id=(there, c), device_id_type=MESH,
            )
            copy.start()
            copies.append(copy)
        return part[pl.ds(pl.multiple_of(s * wide, wide), wide), :], copies

    def weight_total(total, copies, row, ref):
        for d, copy in enumerate(copies):
            copy.wait_recv()
            total = total + recv_part[row, d].astype(jnp.float32)
        ref[...] = (total * scale).T.reshape(ref.shape)

    home, sends = start_gather(got_cot, 0)
    start_pair(halo_copies[0])
    start_pair(halo_copies[1])
    loads[3].wait()
    loads[4].wait()
    pending = forward_gather(got_cot, 0, home, sends)
    pair_two = input_side(w2, got_cot, 0)
    finish_pair(halo_copies[0], hid.at[0], hid.at[2])
    fill(cols_two, hid, -1)
    fill(cols_two, hid, 1)
    total_two, copies_two = weight_side(cols_two, got_cot, 0)

    grad = (input_total(pair_two, 0) * slope[...]).astype(jnp.bfloat16)
    for z in range(nz):
        got_pre[mine, z * ny:(z + 1) * ny] = grad[z * own:(z + 1) * own]
    home, sends = start_gather(got_pre, 1)
    finish_pair(halo_copies[1], layer.at[0], layer.at[2])
    fill(cols_one, layer, -1)
    fill(cols_one, layer, 1)
    weight_total(total_two, copies_two, 0, two_ref)
    pending += forward_gather(got_pre, 1, home, sends)

    total_one, copies_one = weight_side(cols_one, got_pre, 1)
    pair_one = input_side(w1, got_pre, 1)
    out_ref[0] = input_total(pair_one, 1).astype(jnp.bfloat16).reshape(nz, own, ny)
    weight_total(total_one, copies_one, 1, one_ref)

    for copy in pending + copies_two + copies_one:
        copy.wait_send()
    for pair in halo_copies + [pair_two, pair_one]:
        sent_pair(pair)


def solution(mesh):
    ns, groups = mesh.shape["space"], mesh.shape["chan"]

    def shards(layer_input, pre_act, out_grad, weight_one, weight_two):
        _, nz, own, ny = layer_input.shape
        taps, _, chans = weight_one.shape
        scale = float(ns * ny * nz) ** -0.5
        any_space = pl.BlockSpec(memory_space=pl.ANY)
        vmem = pl.BlockSpec(memory_space=pltpu.VMEM)
        bf, f32 = jnp.bfloat16, jnp.float32
        dma = pltpu.SemaphoreType.DMA
        return pl.pallas_call(
            functools.partial(kernel, (ns, nz, own, ny, scale)),
            out_shape=(
                jax.ShapeDtypeStruct(layer_input.shape, bf),
                jax.ShapeDtypeStruct((taps, own, chans // ns), f32),
                jax.ShapeDtypeStruct((taps, own, chans // ns), f32),
            ),
            in_specs=[any_space] * 5,
            out_specs=(vmem, vmem, vmem),
            scratch_shapes=[
                pltpu.VMEM((3, nz, own, ny), bf),
                pltpu.VMEM((nz, own, ny), bf),
                pltpu.VMEM((nz, own, ny), bf),
                pltpu.VMEM(weight_one.shape, bf),
                pltpu.VMEM(weight_two.shape, bf),
                pltpu.VMEM((3, nz, own, ny), bf),
                pltpu.VMEM((nz * own, ny), f32),
                pltpu.VMEM((chans, nz * ny), bf),
                pltpu.VMEM((chans, nz * ny), bf),
                pltpu.VMEM((taps * own, nz * ny), bf),
                pltpu.VMEM((taps * own, nz * ny), bf),
                pltpu.VMEM((taps * own, nz * ny), f32),
                pltpu.VMEM((nz * own, ny), f32),
                pltpu.VMEM((chans, taps * own), f32),
                pltpu.VMEM((2, chans, taps * own), bf),
                pltpu.VMEM((2, ns - 1, chans // ns, taps * own), bf),
                pltpu.VMEM((2, 2, nz, own, ny), bf),
                pltpu.VMEM((2, 2, nz, own, ny), bf),
                dma((5,)),
                dma((2, 7)),
                dma((2, 7)),
                dma((2, 8)),
                dma((2, 8)),
                dma((4,)),
                dma((4,)),
                dma((2, 2)),
                dma((2, 2)),
                dma((2, 7)),
                dma((2, 7)),
            ],
            compiler_params=pltpu.CompilerParams(
                collective_id=0, has_side_effects=True, vmem_limit_bytes=48 * 1024 * 1024
            ),
        )(layer_input, pre_act, out_grad, weight_one, weight_two)

    wide, narrow = P("space", None, "chan", None), P(None, "chan", None)
    return jax.shard_map(
        shards,
        mesh=mesh,
        in_specs=(wide, wide, wide, narrow, narrow),
        out_specs=(wide, P(None, "chan", "space"), P(None, "chan", "space")),
        check_vma=False,
    )
```

```python
import functools

import jax
import jax.numpy as jnp
from jax import lax
from jax.experimental import pallas as pl
from jax.experimental.pallas import tpu as pltpu
from jax.sharding import PartitionSpec as P

MESH = pl.DeviceIdType.MESH
OFFSETS = (-1, 0, 1)
CHIPS = ((2, 2), (2, 0), (1, 2), (3, 2), (1, 0), (3, 0), (0, 2))


def tap(a, b, c):
    return 9 * (a + 1) + 3 * (b + 1) + (c + 1)


def moved(value, step):
    if step == 0:
        return value
    width = value.shape[1]
    lane = lax.broadcasted_iota(jnp.int32, value.shape, 1)
    inside = lane < width - step if step > 0 else lane >= -step
    return jnp.where(inside, pltpu.roll(value, (-step) % width, 1), 0.0)


def kernel(
    dims,
    layer_hbm, pre_hbm, cot_hbm, w1_hbm, w2_hbm,
    out_ref, one_ref, two_ref,
    layer, pre, cot, w1, w2, hid, slope,
    got_cot, got_pre, cols_one, cols_two, prod, center,
    part, send_part, recv_part, send_q, recv_q,
    load_sem, gs, gr, fs, fr, hs, hr, qs, qr, ws, wr,
):
    ns, nz, own, ny, scale = dims
    groups = got_cot.shape[0] // own
    rows = own * nz
    wide = part.shape[0] // ns
    s = lax.axis_index("space")
    c = lax.axis_index("chan")
    zc, wc = lax.div(c, 4), lax.rem(c, 4)
    levels = groups // 4

    def chip(dz, dw):
        return lax.rem(zc + dz, levels) * 4 + (wc ^ dw)

    sibling = (s, c ^ 1)
    mine = pl.ds(pl.multiple_of(c * own, own), own)

    barrier = pltpu.get_barrier_semaphore()
    partners = [(s, chip(*d)) for d in CHIPS] + [(lax.rem(s + d, ns), c) for d in range(1, ns)] + [sibling]
    for p in partners:
        pl.semaphore_signal(barrier, inc=1, device_id=p, device_id_type=MESH)

    loads = [
        pltpu.make_async_copy(src, dst, load_sem.at[k])
        for k, (src, dst) in enumerate(
            ((cot_hbm.at[0], cot), (pre_hbm.at[0], pre), (layer_hbm.at[0], layer.at[1]), (w2_hbm, w2), (w1_hbm, w1))
        )
    ]
    for copy in loads:
        copy.start()

    loads[0].wait()
    for z in range(nz):
        got_cot[mine, z * ny:(z + 1) * ny] = cot[z]
    loads[1].wait()
    value = pre[...].astype(jnp.float32).reshape(rows, ny)
    sig = jax.nn.sigmoid(value)
    hid[1] = (value * sig).astype(jnp.bfloat16).reshape(nz, own, ny)
    slope[...] = sig * (1.0 + value * (1.0 - sig))
    loads[2].wait()

    def fill(cols, field, a):
        plane = field[a + 1].astype(jnp.float32).reshape(rows, ny)
        for b in OFFSETS:
            side = moved(plane, b).astype(jnp.bfloat16)
            for e in OFFSETS:
                k = tap(a, b, e)
                for z in range(nz):
                    if 0 <= z + e < nz:
                        piece = side[(z + e) * own:(z + e + 1) * own]
                    else:
                        piece = jnp.zeros((own, ny), jnp.bfloat16)
                    cols[k * own:(k + 1) * own, z * ny:(z + 1) * ny] = piece

    fill(cols_two, hid, 0)
    fill(cols_one, layer, 0)

    pl.semaphore_wait(barrier, len(partners))

    def start_gather(buf, row):
        home = pltpu.make_async_remote_copy(
            buf.at[mine], buf.at[mine], fs.at[row, 7], fr.at[row, 7], device_id=sibling, device_id_type=MESH
        )
        sends = []
        for k, d in enumerate(CHIPS):
            copy = pltpu.make_async_remote_copy(
                buf.at[mine], buf.at[mine], gs.at[row, k], gr.at[row, k], device_id=(s, chip(*d)), device_id_type=MESH
            )
            copy.start()
            sends.append(copy)
        home.start()
        return home, sends

    def forward_gather(buf, row, home, sends):
        passed = []
        for k in reversed(range(len(CHIPS))):
            dz, dw = CHIPS[k]
            sends[k].wait_recv()
            origin = pl.ds(pl.multiple_of(chip(levels - dz, dw) * own, own), own)
            copy = pltpu.make_async_remote_copy(
                buf.at[origin], buf.at[origin], fs.at[row, k], fr.at[row, k], device_id=sibling, device_id_type=MESH
            )
            copy.start()
            passed.append(copy)
        for copy in [home] + passed:
            copy.wait_recv()
        return [home] + passed + sends

    def halo(src, dst, sem, step, there):
        return pltpu.make_async_remote_copy(
            src, dst, hs.at[sem], hr.at[sem], device_id=(there, c), device_id_type=MESH
        )

    up, down = lax.rem(s + 1, ns), lax.rem(s + ns - 1, ns)

    halo_copies = [
        (halo(hid.at[1], hid.at[0], 0, 1, up), halo(hid.at[1], hid.at[2], 1, -1, down)),
        (halo(layer.at[1], layer.at[0], 2, 1, up), halo(layer.at[1], layer.at[2], 3, -1, down)),
    ]

    def start_pair(pair):
        @pl.when(s < ns - 1)
        def _():
            pair[0].start()

        @pl.when(s > 0)
        def _():
            pair[1].start()

    def finish_pair(pair, low, high):
        @pl.when(s > 0)
        def _():
            pair[0].wait_recv()

        @pl.when(s == 0)
        def _():
            low[...] = jnp.zeros(low.shape, low.dtype)

        @pl.when(s < ns - 1)
        def _():
            pair[1].wait_recv()

        @pl.when(s == ns - 1)
        def _():
            high[...] = jnp.zeros(high.shape, high.dtype)

    def sent_pair(pair):
        @pl.when(s < ns - 1)
        def _():
            pair[0].wait_send()

        @pl.when(s > 0)
        def _():
            pair[1].wait_send()

    def plane_sum(weight, got, a):
        lo = tap(a, -1, -1) * own
        left = weight[9 * (a + 1):9 * (a + 2)].reshape(9 * own, groups * own)
        prod[lo:lo + 9 * own, :] = jnp.dot(left, got[...], preferred_element_type=jnp.float32)
        result = []
        for z in range(nz):
            total = None
            for b in OFFSETS:
                column = None
                for e in OFFSETS:
                    if 0 <= z - e < nz:
                        k = tap(a, b, e)
                        term = prod[k * own:(k + 1) * own, (z - e) * ny:(z - e + 1) * ny]
                        column = term if column is None else column + term
                column = moved(column, -b)
                total = column if total is None else total + column
            result.append(total)
        return result

    def q_pair(row):
        def copy(slot, there):
            return pltpu.make_async_remote_copy(
                send_q.at[row, slot], recv_q.at[row, slot], qs.at[row, slot], qr.at[row, slot],
                device_id=(there, c), device_id_type=MESH,
            )

        return copy(0, up), copy(1, down)

    def input_side(weight, got, row):
        pair = q_pair(row)
        for slot, a in ((0, 1), (1, -1)):
            for z, value in enumerate(plane_sum(weight, got, a)):
                send_q[row, slot, z] = value.astype(jnp.bfloat16)
        start_pair(pair)
        for z, value in enumerate(plane_sum(weight, got, 0)):
            center[z * own:(z + 1) * own, :] = value
        return pair

    def input_total(pair, row):
        finish_pair(pair, recv_q.at[row, 0], recv_q.at[row, 1])
        low = recv_q[row, 0].astype(jnp.float32).reshape(rows, ny)
        high = recv_q[row, 1].astype(jnp.float32).reshape(rows, ny)
        return center[...] + low + high

    def weight_side(cols, got, row):
        part[...] = lax.dot_general(
            got[...], cols[...], (((1,), (1,)), ((), ())), preferred_element_type=jnp.float32
        )
        send_part[row] = part[...].astype(jnp.bfloat16)
        copies = []
        for d in range(1, ns):
            there = lax.rem(s + d, ns)
            block = pl.ds(pl.multiple_of(there * wide, wide), wide)
            copy = pltpu.make_async_remote_copy(
                send_part.at[row, block], recv_part.at[row, d - 1], ws.at[row, d - 1], wr.at[row, d - 1],
                device_id=(there, c), device_id_type=MESH,
            )
            copy.start()
            copies.append(copy)
        return part[pl.ds(pl.multiple_of(s * wide, wide), wide), :], copies

    def weight_total(total, copies, row, ref):
        for d, copy in enumerate(copies):
            copy.wait_recv()
            total = total + recv_part[row, d].astype(jnp.float32)
        ref[...] = (total * scale).T.reshape(ref.shape)

    home, sends = start_gather(got_cot, 0)
    start_pair(halo_copies[0])
    start_pair(halo_copies[1])
    loads[3].wait()
    loads[4].wait()
    pending = forward_gather(got_cot, 0, home, sends)
    pair_two = input_side(w2, got_cot, 0)
    finish_pair(halo_copies[0], hid.at[0], hid.at[2])
    fill(cols_two, hid, -1)
    fill(cols_two, hid, 1)
    total_two, copies_two = weight_side(cols_two, got_cot, 0)

    grad = (input_total(pair_two, 0) * slope[...]).astype(jnp.bfloat16)
    for z in range(nz):
        got_pre[mine, z * ny:(z + 1) * ny] = grad[z * own:(z + 1) * own]
    home, sends = start_gather(got_pre, 1)
    finish_pair(halo_copies[1], layer.at[0], layer.at[2])
    fill(cols_one, layer, -1)
    fill(cols_one, layer, 1)
    weight_total(total_two, copies_two, 0, two_ref)
    pending += forward_gather(got_pre, 1, home, sends)

    total_one, copies_one = weight_side(cols_one, got_pre, 1)
    pair_one = input_side(w1, got_pre, 1)
    out_ref[0] = input_total(pair_one, 1).astype(jnp.bfloat16).reshape(nz, own, ny)
    weight_total(total_one, copies_one, 1, one_ref)

    for copy in pending + copies_two + copies_one:
        copy.wait_send()
    for pair in halo_copies + [pair_two, pair_one]:
        sent_pair(pair)


def hand_out(one_ref, two_ref, three_ref, one_out, two_out, three_out, sem):
    copies = [
        pltpu.make_async_copy(src, dst, sem.at[k])
        for k, (src, dst) in enumerate(((one_ref, one_out), (two_ref, two_out), (three_ref, three_out)))
    ]
    for copy in copies:
        copy.start()
    for copy in copies:
        copy.wait()


def solution(mesh):
    ns, groups = mesh.shape["space"], mesh.shape["chan"]

    def shards(layer_input, pre_act, out_grad, weight_one, weight_two):
        _, nz, own, ny = layer_input.shape
        taps, _, chans = weight_one.shape
        scale = float(ns * ny * nz) ** -0.5
        any_space = pl.BlockSpec(memory_space=pl.ANY)
        vmem = pl.BlockSpec(memory_space=pltpu.VMEM)
        bf, f32 = jnp.bfloat16, jnp.float32
        dma = pltpu.SemaphoreType.DMA
        results = pl.pallas_call(
            functools.partial(kernel, (ns, nz, own, ny, scale)),
            out_shape=(
                jax.ShapeDtypeStruct(layer_input.shape, bf),
                jax.ShapeDtypeStruct((taps, own, chans // ns), f32),
                jax.ShapeDtypeStruct((taps, own, chans // ns), f32),
            ),
            in_specs=[any_space] * 5,
            out_specs=(vmem, vmem, vmem),
            scratch_shapes=[
                pltpu.VMEM((3, nz, own, ny), bf),
                pltpu.VMEM((nz, own, ny), bf),
                pltpu.VMEM((nz, own, ny), bf),
                pltpu.VMEM(weight_one.shape, bf),
                pltpu.VMEM(weight_two.shape, bf),
                pltpu.VMEM((3, nz, own, ny), bf),
                pltpu.VMEM((nz * own, ny), f32),
                pltpu.VMEM((chans, nz * ny), bf),
                pltpu.VMEM((chans, nz * ny), bf),
                pltpu.VMEM((taps * own, nz * ny), bf),
                pltpu.VMEM((taps * own, nz * ny), bf),
                pltpu.VMEM((taps * own, nz * ny), f32),
                pltpu.VMEM((nz * own, ny), f32),
                pltpu.VMEM((chans, taps * own), f32),
                pltpu.VMEM((2, chans, taps * own), bf),
                pltpu.VMEM((2, ns - 1, chans // ns, taps * own), bf),
                pltpu.VMEM((2, 2, nz, own, ny), bf),
                pltpu.VMEM((2, 2, nz, own, ny), bf),
                dma((5,)),
                dma((2, 7)),
                dma((2, 7)),
                dma((2, 8)),
                dma((2, 8)),
                dma((4,)),
                dma((4,)),
                dma((2, 2)),
                dma((2, 2)),
                dma((2, 7)),
                dma((2, 7)),
            ],
            compiler_params=pltpu.CompilerParams(
                collective_id=0, has_side_effects=True, vmem_limit_bytes=48 * 1024 * 1024
            ),
        )(*[pltpu.with_memory_space_constraint(v, pltpu.HBM) for v in (layer_input, pre_act, out_grad, weight_one, weight_two)])
        return pl.pallas_call(
            hand_out,
            out_shape=tuple(jax.ShapeDtypeStruct(v.shape, v.dtype) for v in results),
            in_specs=[vmem] * 3,
            out_specs=(any_space,) * 3,
            scratch_shapes=[dma((3,))],
            compiler_params=pltpu.CompilerParams(vmem_limit_bytes=1024 * 1024),
        )(*results)

    wide, narrow = P("space", None, "chan", None), P(None, "chan", None)
    return jax.shard_map(
        shards,
        mesh=mesh,
        in_specs=(wide, wide, wide, narrow, narrow),
        out_specs=(wide, P(None, "chan", "space"), P(None, "chan", "space")),
        check_vma=False,
    )
```

```python
import functools

import jax
import jax.numpy as jnp
from jax import lax
from jax.experimental import pallas as pl
from jax.experimental.pallas import tpu as pltpu
from jax.sharding import PartitionSpec as P

MESH = pl.DeviceIdType.MESH
OFFSETS = (-1, 0, 1)
CHIPS = ((2, 2), (2, 0), (1, 2), (3, 2), (1, 0), (3, 0), (0, 2))


def tap(a, b, c):
    return 9 * (a + 1) + 3 * (b + 1) + (c + 1)


def moved(value, step):
    if step == 0:
        return value
    width = value.shape[1]
    lane = lax.broadcasted_iota(jnp.int32, value.shape, 1)
    inside = lane < width - step if step > 0 else lane >= -step
    return jnp.where(inside, pltpu.roll(value, (-step) % width, 1), 0.0)


def kernel(
    dims,
    layer_hbm, pre_hbm, cot_hbm, w1_hbm, w2_hbm,
    out_ref, one_ref, two_ref,
    layer, pre, cot, w1, w2, hid, slope,
    got_cot, got_pre, cols_one, cols_two, prod, center,
    part, send_part, recv_part, send_q, recv_q,
    load_sem, gs, gr, fs, fr, hs, hr, qs, qr, ws, wr,
):
    ns, nz, own, ny, scale, (ends_one, ends_two, ends_three) = dims
    groups = got_cot.shape[0] // own
    rows = own * nz
    wide = part.shape[0] // ns
    s = lax.axis_index("space")
    c = lax.axis_index("chan")
    zc, wc = lax.div(c, 4), lax.rem(c, 4)
    levels = groups // 4

    def chip(dz, dw):
        return lax.rem(zc + dz, levels) * 4 + (wc ^ dw)

    sibling = (s, c ^ 1)
    mine = pl.ds(pl.multiple_of(c * own, own), own)

    barrier = pltpu.get_barrier_semaphore()
    partners = [(s, chip(*d)) for d in CHIPS] + [(lax.rem(s + d, ns), c) for d in range(1, ns)] + [sibling]
    for p in partners:
        pl.semaphore_signal(barrier, inc=1, device_id=p, device_id_type=MESH)

    loads = [
        pltpu.make_async_copy(src, dst, load_sem.at[k])
        for k, (src, dst) in enumerate(
            ((cot_hbm.at[0], cot), (pre_hbm.at[0], pre), (layer_hbm.at[0], layer.at[1]), (w2_hbm, w2), (w1_hbm, w1))
        )
    ]
    for copy in loads:
        copy.start()

    loads[0].wait()
    for z in range(nz):
        got_cot[mine, z * ny:(z + 1) * ny] = cot[z]
    pl.semaphore_wait(barrier, len(partners))

    def lanes(j, ends):
        start = ends[j - 1] if j else 0
        return pl.ds(start * ny, (ends[j] - start) * ny)

    def start_gather(buf, row, j, ends):
        span = lanes(j, ends)
        sends = []
        for k, d in enumerate(CHIPS):
            copy = pltpu.make_async_remote_copy(
                buf.at[mine, span], buf.at[mine, span], gs.at[row, j, k], gr.at[row, j, k],
                device_id=(s, chip(*d)), device_id_type=MESH,
            )
            copy.start()
            sends.append(copy)
        home = pltpu.make_async_remote_copy(
            buf.at[mine, span], buf.at[mine, span], fs.at[row, j, len(CHIPS)], fr.at[row, j, len(CHIPS)],
            device_id=sibling, device_id_type=MESH,
        )
        home.start()
        return home, sends

    def forward_gather(buf, row, j, ends, home, sends):
        span = lanes(j, ends)
        passed = []
        for k in reversed(range(len(CHIPS))):
            dz, dw = CHIPS[k]
            sends[k].wait_recv()
            origin = pl.ds(pl.multiple_of(chip(levels - dz, dw) * own, own), own)
            copy = pltpu.make_async_remote_copy(
                buf.at[origin, span], buf.at[origin, span], fs.at[row, j, k], fr.at[row, j, k],
                device_id=sibling, device_id_type=MESH,
            )
            copy.start()
            passed.append(copy)
        for copy in [home] + passed:
            copy.wait_recv()
        return [home] + passed + sends

    def halo(src, dst, sem, there):
        return pltpu.make_async_remote_copy(
            src, dst, hs.at[sem], hr.at[sem], device_id=(there, c), device_id_type=MESH
        )

    up, down = lax.rem(s + 1, ns), lax.rem(s + ns - 1, ns)

    def start_pair(pair):
        @pl.when(s < ns - 1)
        def _():
            pair[0].start()

        @pl.when(s > 0)
        def _():
            pair[1].start()

    def finish_pair(pair, low, high):
        @pl.when(s > 0)
        def _():
            pair[0].wait_recv()

        @pl.when(s == 0)
        def _():
            low[...] = jnp.zeros(low.shape, low.dtype)

        @pl.when(s < ns - 1)
        def _():
            pair[1].wait_recv()

        @pl.when(s == ns - 1)
        def _():
            high[...] = jnp.zeros(high.shape, high.dtype)

    def sent_pair(pair):
        @pl.when(s < ns - 1)
        def _():
            pair[0].wait_send()

        @pl.when(s > 0)
        def _():
            pair[1].wait_send()

    def fill(cols, field, a):
        plane = field[a + 1].astype(jnp.float32).reshape(rows, ny)
        for b in OFFSETS:
            side = moved(plane, b).astype(jnp.bfloat16)
            for e in OFFSETS:
                k = tap(a, b, e)
                for z in range(nz):
                    if 0 <= z + e < nz:
                        piece = side[(z + e) * own:(z + e + 1) * own]
                    else:
                        piece = jnp.zeros((own, ny), jnp.bfloat16)
                    cols[k * own:(k + 1) * own, z * ny:(z + 1) * ny] = piece

    def plane_sum(a, first, last):
        for z in range(first, last):
            total = None
            for b in OFFSETS:
                column = None
                for e in OFFSETS:
                    if 0 <= z - e < nz:
                        k = tap(a, b, e)
                        term = prod[k * own:(k + 1) * own, (z - e) * ny:(z - e + 1) * ny]
                        column = term if column is None else column + term
                column = moved(column, -b)
                total = column if total is None else total + column
            yield z, total

    def input_side(weight, got, row, j, ends_in, ends_out):
        span = lanes(j, ends_in)
        first, last = (ends_out[j - 1] if j else 0), ends_out[j]
        field = got[:, span]

        def product(a):
            lo = tap(a, -1, -1) * own
            left = weight[9 * (a + 1):9 * (a + 2)].reshape(9 * own, groups * own)
            prod[lo:lo + 9 * own, span] = jnp.dot(left, field, preferred_element_type=jnp.float32)

        def copy(slot, there):
            part_z = pl.ds(first, last - first)
            return pltpu.make_async_remote_copy(
                send_q.at[row, slot, part_z], recv_q.at[row, slot, part_z], qs.at[row, j, slot], qr.at[row, j, slot],
                device_id=(there, c), device_id_type=MESH,
            )

        pair = copy(0, up), copy(1, down)
        for slot, a in ((0, 1), (1, -1)):
            product(a)
            for z, value in plane_sum(a, first, last):
                send_q[row, slot, z] = value.astype(jnp.bfloat16)
        start_pair(pair)
        product(0)
        for z, value in plane_sum(0, first, last):
            center[z * own:(z + 1) * own, :] = value
        return pair

    def input_total(pair, row, j, ends):
        first, last = (ends[j - 1] if j else 0), ends[j]
        part_z = pl.ds(first, last - first)
        finish_pair(pair, recv_q.at[row, 0, part_z], recv_q.at[row, 1, part_z])
        low = recv_q[row, 0, first:last].astype(jnp.float32).reshape((last - first) * own, ny)
        high = recv_q[row, 1, first:last].astype(jnp.float32).reshape((last - first) * own, ny)
        return first, last, center[first * own:last * own, :] + low + high

    def weight_product(cols, got, span):
        return lax.dot_general(
            got[:, span], cols[:, span], (((1,), (1,)), ((), ())), preferred_element_type=jnp.float32
        )

    def weight_pack(row):
        send_part[row] = part[...].astype(jnp.bfloat16)
        return part[pl.ds(pl.multiple_of(s * wide, wide), wide), :]

    def weight_send(row):
        copies = []
        for d in range(1, ns):
            there = lax.rem(s + d, ns)
            block = pl.ds(pl.multiple_of(there * wide, wide), wide)
            copy = pltpu.make_async_remote_copy(
                send_part.at[row, block], recv_part.at[row, d - 1], ws.at[row, d - 1], wr.at[row, d - 1],
                device_id=(there, c), device_id_type=MESH,
            )
            copy.start()
            copies.append(copy)
        return copies

    def weight_total(total, copies, row, ref):
        for d, copy in enumerate(copies):
            copy.wait_recv()
            total = total + recv_part[row, d].astype(jnp.float32)
        ref[...] = (total * scale).T.reshape(ref.shape)

    chunks = len(ends_one)
    started = [start_gather(got_cot, 0, j, ends_one) for j in range(chunks)]

    loads[1].wait()
    value = pre[...].astype(jnp.float32).reshape(rows, ny)
    sig = jax.nn.sigmoid(value)
    hid[1] = (value * sig).astype(jnp.bfloat16).reshape(nz, own, ny)
    slope[...] = sig * (1.0 + value * (1.0 - sig))
    loads[2].wait()
    halo_copies = [
        (halo(hid.at[1], hid.at[0], 0, up), halo(hid.at[1], hid.at[2], 1, down)),
        (halo(layer.at[1], layer.at[0], 2, up), halo(layer.at[1], layer.at[2], 3, down)),
    ]
    start_pair(halo_copies[0])
    start_pair(halo_copies[1])
    fill(cols_two, hid, 0)
    fill(cols_one, layer, 0)
    loads[3].wait()
    loads[4].wait()

    pending, pairs = [], []
    for j in range(chunks):
        pending += forward_gather(got_cot, 0, j, ends_one, *started[j])
        pairs.append(input_side(w2, got_cot, 0, j, ends_one, ends_two))
    started = []
    for j in range(chunks):
        first, last, grad = input_total(pairs[j], 0, j, ends_two)
        grad = (grad * slope[first * own:last * own, :]).astype(jnp.bfloat16)
        for z in range(first, last):
            got_pre[mine, z * ny:(z + 1) * ny] = grad[(z - first) * own:(z - first + 1) * own]
        started.append(start_gather(got_pre, 1, j, ends_two))
    finish_pair(halo_copies[0], hid.at[0], hid.at[2])
    fill(cols_two, hid, -1)
    fill(cols_two, hid, 1)
    part[...] = weight_product(cols_two, got_cot, pl.ds(0, nz * ny))
    total_two = weight_pack(0)

    finish_pair(halo_copies[1], layer.at[0], layer.at[2])
    fill(cols_one, layer, -1)
    fill(cols_one, layer, 1)

    for j in range(chunks):
        pending += forward_gather(got_pre, 1, j, ends_two, *started[j])
        if j == 0:
            copies_two = weight_send(0)
        piece = weight_product(cols_one, got_pre, lanes(j, ends_two))
        part[...] = piece if j == 0 else part[...] + piece
        if j == chunks - 1:
            total_one = weight_pack(1)
            copies_one = weight_send(1)
        pairs.append(input_side(w1, got_pre, 1, j, ends_two, ends_three))
    weight_total(total_two, copies_two, 0, two_ref)
    for j in range(chunks):
        first, last, grad = input_total(pairs[chunks + j], 1, j, ends_three)
        out_ref[0, first:last] = grad.astype(jnp.bfloat16).reshape(last - first, own, ny)
    weight_total(total_one, copies_one, 1, one_ref)

    for copy in pending + copies_two + copies_one:
        copy.wait_send()
    for pair in halo_copies + pairs:
        sent_pair(pair)


def hand_out(one_ref, two_ref, three_ref, one_out, two_out, three_out, sem):
    copies = [
        pltpu.make_async_copy(src, dst, sem.at[k])
        for k, (src, dst) in enumerate(((one_ref, one_out), (two_ref, two_out), (three_ref, three_out)))
    ]
    for copy in copies:
        copy.start()
    for copy in copies:
        copy.wait()


def solution(mesh):
    ns, groups = mesh.shape["space"], mesh.shape["chan"]

    def shards(layer_input, pre_act, out_grad, weight_one, weight_two):
        _, nz, own, ny = layer_input.shape
        taps, _, chans = weight_one.shape
        scale = float(ns * ny * nz) ** -0.5
        chunks = 2
        ends = tuple(
            tuple(nz if j == chunks - 1 else nz * (j + 1) // chunks + shift for j in range(chunks)) for shift in (1, 0, -1)
        )
        any_space = pl.BlockSpec(memory_space=pl.ANY)
        vmem = pl.BlockSpec(memory_space=pltpu.VMEM)
        bf, f32 = jnp.bfloat16, jnp.float32
        dma = pltpu.SemaphoreType.DMA
        results = pl.pallas_call(
            functools.partial(kernel, (ns, nz, own, ny, scale, ends)),
            out_shape=(
                jax.ShapeDtypeStruct(layer_input.shape, bf),
                jax.ShapeDtypeStruct((taps, own, chans // ns), f32),
                jax.ShapeDtypeStruct((taps, own, chans // ns), f32),
            ),
            in_specs=[any_space] * 5,
            out_specs=(vmem, vmem, vmem),
            scratch_shapes=[
                pltpu.VMEM((3, nz, own, ny), bf),
                pltpu.VMEM((nz, own, ny), bf),
                pltpu.VMEM((nz, own, ny), bf),
                pltpu.VMEM(weight_one.shape, bf),
                pltpu.VMEM(weight_two.shape, bf),
                pltpu.VMEM((3, nz, own, ny), bf),
                pltpu.VMEM((nz * own, ny), f32),
                pltpu.VMEM((chans, nz * ny), bf),
                pltpu.VMEM((chans, nz * ny), bf),
                pltpu.VMEM((taps * own, nz * ny), bf),
                pltpu.VMEM((taps * own, nz * ny), bf),
                pltpu.VMEM((taps * own, nz * ny), f32),
                pltpu.VMEM((nz * own, ny), f32),
                pltpu.VMEM((chans, taps * own), f32),
                pltpu.VMEM((2, chans, taps * own), bf),
                pltpu.VMEM((2, ns - 1, chans // ns, taps * own), bf),
                pltpu.VMEM((2, 2, nz, own, ny), bf),
                pltpu.VMEM((2, 2, nz, own, ny), bf),
                dma((5,)),
                dma((2, chunks, len(CHIPS))),
                dma((2, chunks, len(CHIPS))),
                dma((2, chunks, len(CHIPS) + 1)),
                dma((2, chunks, len(CHIPS) + 1)),
                dma((4,)),
                dma((4,)),
                dma((2, chunks, 2)),
                dma((2, chunks, 2)),
                dma((2, ns - 1)),
                dma((2, ns - 1)),
            ],
            compiler_params=pltpu.CompilerParams(
                collective_id=0, has_side_effects=True, vmem_limit_bytes=48 * 1024 * 1024
            ),
        )(*[pltpu.with_memory_space_constraint(v, pltpu.HBM) for v in (layer_input, pre_act, out_grad, weight_one, weight_two)])
        return pl.pallas_call(
            hand_out,
            out_shape=tuple(jax.ShapeDtypeStruct(v.shape, v.dtype) for v in results),
            in_specs=[vmem] * 3,
            out_specs=(any_space,) * 3,
            scratch_shapes=[dma((3,))],
            compiler_params=pltpu.CompilerParams(vmem_limit_bytes=1024 * 1024),
        )(*results)

    wide, narrow = P("space", None, "chan", None), P(None, "chan", None)
    return jax.shard_map(
        shards,
        mesh=mesh,
        in_specs=(wide, wide, wide, narrow, narrow),
        out_specs=(wide, P(None, "chan", "space"), P(None, "chan", "space")),
        check_vma=False,
    )
```

```python
import functools

import jax
import jax.numpy as jnp
from jax import lax
from jax.experimental import pallas as pl
from jax.experimental.pallas import tpu as pltpu
from jax.sharding import PartitionSpec as P

MESH = pl.DeviceIdType.MESH
OFFSETS = (-1, 0, 1)
CHIPS = ((2, 2), (2, 0), (1, 2), (3, 2), (1, 0), (3, 0), (0, 2))


DISTANCES = (2, 6, 1, 3, 5, 7, 4)


def tap(a, b, c):
    return 9 * (a + 1) + 3 * (b + 1) + (c + 1)


def moved(value, step):
    if step == 0:
        return value
    width = value.shape[1]
    lane = lax.broadcasted_iota(jnp.int32, value.shape, 1)
    inside = lane < width - step if step > 0 else lane >= -step
    return jnp.where(inside, pltpu.roll(value, (-step) % width, 1), 0.0)


def kernel(
    dims,
    layer_hbm, pre_hbm, cot_hbm, w1_hbm, w2_hbm,
    out_ref, one_ref, two_ref,
    layer, pre, cot, w1, w2, hid, slope,
    got_cot, got_pre, cols_one, cols_two, prod, center,
    part, send_part, recv_part, near, line_sum, line_send, opposite, send_q, recv_q,
    load_sem, gs, gr, fs, fr, hs, hr, qs, qr, ws, wr, ns_sem, nr_sem, os_sem, or_sem,
):
    ns, nz, own, ny, scale, (ends_one, ends_two, ends_three) = dims
    groups = got_cot.shape[0] // own
    rows = own * nz
    line = ns // 2
    taps = w1.shape[0]
    wide = part.shape[0] // ns
    s = lax.axis_index("space")
    c = lax.axis_index("chan")
    zc, wc = lax.div(c, 4), lax.rem(c, 4)
    levels = groups // 4

    def chip(dz, dw):
        return lax.rem(zc + dz, levels) * 4 + (wc ^ dw)

    sibling = (s, c ^ 1)
    mine = pl.ds(pl.multiple_of(c * own, own), own)

    barrier = pltpu.get_barrier_semaphore()
    partners = [(s, chip(*d)) for d in CHIPS] + [(lax.rem(s + d, ns), c) for d in range(1, ns)] + [sibling]
    for p in partners:
        pl.semaphore_signal(barrier, inc=1, device_id=p, device_id_type=MESH)

    loads = [
        pltpu.make_async_copy(src, dst, load_sem.at[k])
        for k, (src, dst) in enumerate(
            ((cot_hbm.at[0], cot), (pre_hbm.at[0], pre), (layer_hbm.at[0], layer.at[1]), (w2_hbm, w2), (w1_hbm, w1))
        )
    ]
    for copy in loads:
        copy.start()

    loads[0].wait()
    for z in range(nz):
        got_cot[mine, z * ny:(z + 1) * ny] = cot[z]
    pl.semaphore_wait(barrier, len(partners))

    def lanes(j, ends):
        start = ends[j - 1] if j else 0
        return pl.ds(start * ny, (ends[j] - start) * ny)

    def start_gather(buf, row, j, ends):
        span = lanes(j, ends)
        sends = []
        for k, d in enumerate(CHIPS):
            copy = pltpu.make_async_remote_copy(
                buf.at[mine, span], buf.at[mine, span], gs.at[row, j, k], gr.at[row, j, k],
                device_id=(s, chip(*d)), device_id_type=MESH,
            )
            copy.start()
            sends.append(copy)
        home = pltpu.make_async_remote_copy(
            buf.at[mine, span], buf.at[mine, span], fs.at[row, j, len(CHIPS)], fr.at[row, j, len(CHIPS)],
            device_id=sibling, device_id_type=MESH,
        )
        home.start()
        return home, sends

    def forward_gather(buf, row, j, ends, home, sends):
        span = lanes(j, ends)
        passed = []
        for k in reversed(range(len(CHIPS))):
            dz, dw = CHIPS[k]
            sends[k].wait_recv()
            origin = pl.ds(pl.multiple_of(chip(levels - dz, dw) * own, own), own)
            copy = pltpu.make_async_remote_copy(
                buf.at[origin, span], buf.at[origin, span], fs.at[row, j, k], fr.at[row, j, k],
                device_id=sibling, device_id_type=MESH,
            )
            copy.start()
            passed.append(copy)
        for copy in [home] + passed:
            copy.wait_recv()
        return [home] + passed + sends

    def halo(src, dst, sem, there):
        return pltpu.make_async_remote_copy(
            src, dst, hs.at[sem], hr.at[sem], device_id=(there, c), device_id_type=MESH
        )

    up, down = lax.rem(s + 1, ns), lax.rem(s + ns - 1, ns)

    def start_pair(pair):
        @pl.when(s < ns - 1)
        def _():
            pair[0].start()

        @pl.when(s > 0)
        def _():
            pair[1].start()

    def finish_pair(pair, low, high):
        @pl.when(s > 0)
        def _():
            pair[0].wait_recv()

        @pl.when(s == 0)
        def _():
            low[...] = jnp.zeros(low.shape, low.dtype)

        @pl.when(s < ns - 1)
        def _():
            pair[1].wait_recv()

        @pl.when(s == ns - 1)
        def _():
            high[...] = jnp.zeros(high.shape, high.dtype)

    def sent_pair(pair):
        @pl.when(s < ns - 1)
        def _():
            pair[0].wait_send()

        @pl.when(s > 0)
        def _():
            pair[1].wait_send()

    def fill(cols, field, a):
        plane = field[a + 1].astype(jnp.float32).reshape(rows, ny)
        for b in OFFSETS:
            side = moved(plane, b).astype(jnp.bfloat16)
            for e in OFFSETS:
                k = tap(a, b, e)
                for z in range(nz):
                    if 0 <= z + e < nz:
                        piece = side[(z + e) * own:(z + e + 1) * own]
                    else:
                        piece = jnp.zeros((own, ny), jnp.bfloat16)
                    cols[k * own:(k + 1) * own, z * ny:(z + 1) * ny] = piece

    def plane_sum(a, first, last):
        for z in range(first, last):
            total = None
            for b in OFFSETS:
                column = None
                for e in OFFSETS:
                    if 0 <= z - e < nz:
                        k = tap(a, b, e)
                        term = prod[k * own:(k + 1) * own, (z - e) * ny:(z - e + 1) * ny]
                        column = term if column is None else column + term
                column = moved(column, -b)
                total = column if total is None else total + column
            yield z, total

    def input_side(weight, got, row, j, ends_in, ends_out):
        span = lanes(j, ends_in)
        first, last = (ends_out[j - 1] if j else 0), ends_out[j]
        field = got[:, span]

        def product(a):
            lo = tap(a, -1, -1) * own
            left = weight[9 * (a + 1):9 * (a + 2)].reshape(9 * own, groups * own)
            prod[lo:lo + 9 * own, span] = jnp.dot(left, field, preferred_element_type=jnp.float32)

        def copy(slot, there):
            part_z = pl.ds(first, last - first)
            return pltpu.make_async_remote_copy(
                send_q.at[row, slot, part_z], recv_q.at[row, slot, part_z], qs.at[row, j, slot], qr.at[row, j, slot],
                device_id=(there, c), device_id_type=MESH,
            )

        pair = copy(0, up), copy(1, down)
        for slot, a in ((0, 1), (1, -1)):
            product(a)
            for z, value in plane_sum(a, first, last):
                send_q[row, slot, z] = value.astype(jnp.bfloat16)

            @pl.when((s < ns - 1) if slot == 0 else (s > 0))
            def _():
                pair[slot].start()
        product(0)
        for z, value in plane_sum(0, first, last):
            center[z * own:(z + 1) * own, :] = value
        return pair

    def input_total(pair, row, j, ends):
        first, last = (ends[j - 1] if j else 0), ends[j]
        part_z = pl.ds(first, last - first)
        finish_pair(pair, recv_q.at[row, 0, part_z], recv_q.at[row, 1, part_z])
        low = recv_q[row, 0, first:last].astype(jnp.float32).reshape((last - first) * own, ny)
        high = recv_q[row, 1, first:last].astype(jnp.float32).reshape((last - first) * own, ny)
        return first, last, center[first * own:last * own, :] + low + high

    def weight_product(cols, got, span):
        return lax.dot_general(
            got[:, span], cols[:, span], (((1,), (1,)), ((), ())), preferred_element_type=jnp.float32
        )

    def weight_pack(row):
        send_part[row] = part[...].astype(jnp.bfloat16)
        return part[pl.ds(pl.multiple_of(s * wide, wide), wide), :]

    def weight_send(row):
        copies = []
        for d in DISTANCES:
            there = lax.rem(s + d, ns)
            block = pl.ds(pl.multiple_of(there * wide, wide), wide)
            copy = pltpu.make_async_remote_copy(
                send_part.at[row, block], recv_part.at[row, d - 1], ws.at[row, d - 1], wr.at[row, d - 1],
                device_id=(there, c), device_id_type=MESH,
            )
            copy.start()
            copies.append(copy)
        return copies

    side = lax.div(s, line)

    def near_send():
        copies = []
        for d in (2, 1, 3):
            place = lax.rem(s + d, line)
            for e in range(2):
                block = pl.ds(pl.multiple_of((e * line + place) * wide, wide), wide)
                copies.append(pltpu.make_async_remote_copy(
                    send_part.at[0, block], near.at[d - 1, e], ns_sem.at[d - 1, e], nr_sem.at[d - 1, e],
                    device_id=(side * line + place, c), device_id_type=MESH,
                ))
        for copy in copies:
            copy.start()
        own_parts = [
            part[pl.ds(pl.multiple_of((e * line + lax.rem(s, line)) * wide, wide), wide), :] for e in range(2)
        ]
        for e in range(2):
            line_sum[e] = own_parts[e]
        return copies

    def across_send(copies):
        for copy in copies:
            copy.wait_recv()
        for e in range(2):
            total = line_sum[e]
            for d in range(line - 1):
                total = total + near[d, e].astype(jnp.float32)
            line_sum[e] = total
            line_send[e] = total.astype(jnp.bfloat16)
        copy = pltpu.make_async_remote_copy(
            line_send.at[1 - side], opposite, os_sem, or_sem,
            device_id=((1 - side) * line + lax.rem(s, line), c), device_id_type=MESH,
        )
        copy.start()
        return copy

    def across_total(copy, ref):
        copy.wait_recv()
        total = line_sum[side] + opposite[...].astype(jnp.float32)
        ref[...] = (total[:, :taps * own] * scale).T.reshape(ref.shape)

    def weight_total(total, copies, row, ref):
        for d, copy in zip(DISTANCES, copies):
            copy.wait_recv()
            total = total + recv_part[row, d - 1].astype(jnp.float32)
        ref[...] = (total[:, :taps * own] * scale).T.reshape(ref.shape)

    chunks = len(ends_one)
    started = [start_gather(got_cot, 0, j, ends_one) for j in range(chunks)]

    loads[1].wait()
    value = pre[...].astype(jnp.float32).reshape(rows, ny)
    sig = jax.nn.sigmoid(value)
    hid[1] = (value * sig).astype(jnp.bfloat16).reshape(nz, own, ny)
    slope[...] = sig * (1.0 + value * (1.0 - sig))
    loads[2].wait()
    halo_copies = [
        (halo(hid.at[1], hid.at[0], 0, up), halo(hid.at[1], hid.at[2], 1, down)),
        (halo(layer.at[1], layer.at[0], 2, up), halo(layer.at[1], layer.at[2], 3, down)),
    ]
    for cols in (cols_two, cols_one):
        cols[taps * own:, :] = jnp.zeros((cols.shape[0] - taps * own, nz * ny), jnp.bfloat16)
    fill(cols_two, hid, 0)
    fill(cols_one, layer, 0)
    loads[3].wait()
    loads[4].wait()

    pending, pairs = [], []
    for j in range(chunks):
        pending += forward_gather(got_cot, 0, j, ends_one, *started[j])
        pairs.append(input_side(w2, got_cot, 0, j, ends_one, ends_two))
    start_pair(halo_copies[0])
    start_pair(halo_copies[1])
    started = []
    for j in range(chunks):
        first, last, grad = input_total(pairs[j], 0, j, ends_two)
        grad = (grad * slope[first * own:last * own, :]).astype(jnp.bfloat16)
        for z in range(first, last):
            got_pre[mine, z * ny:(z + 1) * ny] = grad[(z - first) * own:(z - first + 1) * own]
        started.append(start_gather(got_pre, 1, j, ends_two))
    finish_pair(halo_copies[0], hid.at[0], hid.at[2])
    fill(cols_two, hid, -1)
    fill(cols_two, hid, 1)
    part[...] = weight_product(cols_two, got_cot, pl.ds(0, nz * ny))
    weight_pack(0)
    near_copies = near_send()

    finish_pair(halo_copies[1], layer.at[0], layer.at[2])
    fill(cols_one, layer, -1)
    fill(cols_one, layer, 1)

    for j in range(chunks):
        pending += forward_gather(got_pre, 1, j, ends_two, *started[j])
        piece = weight_product(cols_one, got_pre, lanes(j, ends_two))
        part[...] = piece if j == 0 else part[...] + piece
        if j == chunks - 1:
            total_one = weight_pack(1)
            copies_one = weight_send(1)
        pairs.append(input_side(w1, got_pre, 1, j, ends_two, ends_three))
    across = across_send(near_copies)
    for j in range(chunks):
        first, last, grad = input_total(pairs[chunks + j], 1, j, ends_three)
        out_ref[0, first:last] = grad.astype(jnp.bfloat16).reshape(last - first, own, ny)
    across_total(across, two_ref)
    weight_total(total_one, copies_one, 1, one_ref)

    for copy in pending + near_copies + [across] + copies_one:
        copy.wait_send()
    for pair in halo_copies + pairs:
        sent_pair(pair)


def hand_out(one_ref, two_ref, three_ref, one_out, two_out, three_out, sem):
    copies = [
        pltpu.make_async_copy(src, dst, sem.at[k])
        for k, (src, dst) in enumerate(((one_ref, one_out), (two_ref, two_out), (three_ref, three_out)))
    ]
    for copy in copies:
        copy.start()
    for copy in copies:
        copy.wait()


def solution(mesh):
    ns, groups = mesh.shape["space"], mesh.shape["chan"]

    def shards(layer_input, pre_act, out_grad, weight_one, weight_two):
        _, nz, own, ny = layer_input.shape
        taps, _, chans = weight_one.shape
        padded = -(-taps * own // 128) * 128
        scale = float(ns * ny * nz) ** -0.5
        chunks = 2
        ends = tuple(
            tuple(nz if j == chunks - 1 else nz * (j + 1) // chunks + shift for j in range(chunks)) for shift in (1, 0, -1)
        )
        any_space = pl.BlockSpec(memory_space=pl.ANY)
        vmem = pl.BlockSpec(memory_space=pltpu.VMEM)
        bf, f32 = jnp.bfloat16, jnp.float32
        dma = pltpu.SemaphoreType.DMA
        results = pl.pallas_call(
            functools.partial(kernel, (ns, nz, own, ny, scale, ends)),
            out_shape=(
                jax.ShapeDtypeStruct(layer_input.shape, bf),
                jax.ShapeDtypeStruct((taps, own, chans // ns), f32),
                jax.ShapeDtypeStruct((taps, own, chans // ns), f32),
            ),
            in_specs=[any_space] * 5,
            out_specs=(vmem, vmem, vmem),
            scratch_shapes=[
                pltpu.VMEM((3, nz, own, ny), bf),
                pltpu.VMEM((nz, own, ny), bf),
                pltpu.VMEM((nz, own, ny), bf),
                pltpu.VMEM(weight_one.shape, bf),
                pltpu.VMEM(weight_two.shape, bf),
                pltpu.VMEM((3, nz, own, ny), bf),
                pltpu.VMEM((nz * own, ny), f32),
                pltpu.VMEM((chans, nz * ny), bf),
                pltpu.VMEM((chans, nz * ny), bf),
                pltpu.VMEM((padded, nz * ny), bf),
                pltpu.VMEM((padded, nz * ny), bf),
                pltpu.VMEM((taps * own, nz * ny), f32),
                pltpu.VMEM((nz * own, ny), f32),
                pltpu.VMEM((chans, padded), f32),
                pltpu.VMEM((2, chans, padded), bf),
                pltpu.VMEM((2, ns - 1, chans // ns, padded), bf),
                pltpu.VMEM((ns // 2 - 1, 2, chans // ns, padded), bf),
                pltpu.VMEM((2, chans // ns, padded), f32),
                pltpu.VMEM((2, chans // ns, padded), bf),
                pltpu.VMEM((chans // ns, padded), bf),
                pltpu.VMEM((2, 2, nz, own, ny), bf),
                pltpu.VMEM((2, 2, nz, own, ny), bf),
                dma((5,)),
                dma((2, chunks, len(CHIPS))),
                dma((2, chunks, len(CHIPS))),
                dma((2, chunks, len(CHIPS) + 1)),
                dma((2, chunks, len(CHIPS) + 1)),
                dma((4,)),
                dma((4,)),
                dma((2, chunks, 2)),
                dma((2, chunks, 2)),
                dma((2, ns - 1)),
                dma((2, ns - 1)),
                dma((ns // 2 - 1, 2)),
                dma((ns // 2 - 1, 2)),
                dma,
                dma,
            ],
            compiler_params=pltpu.CompilerParams(
                collective_id=0, has_side_effects=True, vmem_limit_bytes=48 * 1024 * 1024
            ),
        )(*[pltpu.with_memory_space_constraint(v, pltpu.HBM) for v in (layer_input, pre_act, out_grad, weight_one, weight_two)])
        return pl.pallas_call(
            hand_out,
            out_shape=tuple(jax.ShapeDtypeStruct(v.shape, v.dtype) for v in results),
            in_specs=[vmem] * 3,
            out_specs=(any_space,) * 3,
            scratch_shapes=[dma((3,))],
            compiler_params=pltpu.CompilerParams(vmem_limit_bytes=1024 * 1024),
        )(*results)

    wide, narrow = P("space", None, "chan", None), P(None, "chan", None)
    return jax.shard_map(
        shards,
        mesh=mesh,
        in_specs=(wide, wide, wide, narrow, narrow),
        out_specs=(wide, P(None, "chan", "space"), P(None, "chan", "space")),
        check_vma=False,
    )
```

```python
import functools

import jax
import jax.numpy as jnp
from jax import lax
from jax.experimental import pallas as pl
from jax.experimental.pallas import tpu as pltpu
from jax.sharding import PartitionSpec as P

MESH = pl.DeviceIdType.MESH
OFFSETS = (-1, 0, 1)
CHIPS = ((2, 2), (2, 0), (1, 2), (3, 2), (1, 0), (3, 0), (0, 2))


GROUPS = (0, 3, 1, 2)
DISTANCES = (2, 6, 1, 3, 5, 7, 4)


def tap(a, b, c):
    return 9 * (a + 1) + 3 * (b + 1) + (c + 1)


def moved(value, step):
    if step == 0:
        return value
    width = value.shape[1]
    lane = lax.broadcasted_iota(jnp.int32, value.shape, 1)
    inside = lane < width - step if step > 0 else lane >= -step
    return jnp.where(inside, pltpu.roll(value, (-step) % width, 1), 0.0)


def kernel(
    dims,
    layer_hbm, pre_hbm, cot_hbm, w1_hbm, w2_hbm,
    out_ref, one_ref, two_ref,
    layer, pre, cot, w1, w2, ordered_one, ordered_two, hid, slope,
    got_cot, got_pre, cols_one, cols_two, prod, center,
    part, send_part, recv_part, near, line_sum, line_send, opposite, send_q, recv_q,
    load_sem, gs, gr, fs, fr, hs, hr, qs, qr, ws, wr, ns_sem, nr_sem, os_sem, or_sem,
):
    ns, nz, own, ny, scale, (ends_one, ends_two, ends_three) = dims
    groups = got_cot.shape[0] // own
    rows = own * nz
    line = ns // 2
    taps = w1.shape[0]
    s = lax.axis_index("space")
    c = lax.axis_index("chan")
    zc, wc = lax.div(c, 4), lax.rem(c, 4)
    levels = groups // 4

    def chip(dz, dw):
        return lax.rem(zc + dz, levels) * 4 + (wc ^ dw)

    sibling = (s, c ^ 1)
    core, half = lax.rem(c, 2), got_cot.shape[0] // 2
    mine = pl.ds(pl.multiple_of(core * half + lax.div(c, 2) * own, own), own)

    barrier = pltpu.get_barrier_semaphore()
    partners = [(s, chip(*d)) for d in CHIPS] + [(lax.rem(s + d, ns), c) for d in range(1, ns)] + [sibling]
    for p in partners:
        pl.semaphore_signal(barrier, inc=1, device_id=p, device_id_type=MESH)

    loads = [
        pltpu.make_async_copy(src, dst, load_sem.at[k])
        for k, (src, dst) in enumerate(
            ((cot_hbm.at[0], cot), (pre_hbm.at[0], pre), (layer_hbm.at[0], layer.at[1]), (w2_hbm, w2), (w1_hbm, w1))
        )
    ]
    for copy in loads:
        copy.start()

    loads[0].wait()
    for z in range(nz):
        got_cot[mine, z * ny:(z + 1) * ny] = cot[z]
    pl.semaphore_wait(barrier, len(partners))

    def lanes(j, ends):
        start = ends[j - 1] if j else 0
        return pl.ds(start * ny, (ends[j] - start) * ny)

    def start_gather(buf, row, j, ends):
        span = lanes(j, ends)
        sends = []
        for k, d in enumerate(CHIPS):
            copy = pltpu.make_async_remote_copy(
                buf.at[mine, span], buf.at[mine, span], gs.at[row, j, k], gr.at[row, j, k],
                device_id=(s, chip(*d)), device_id_type=MESH,
            )
            copy.start()
            sends.append(copy)
        return sends

    def forward_gather(buf, row, j, ends, sends):
        span = lanes(j, ends)
        passed = []
        for g in GROUPS:
            for k, (dz, _) in enumerate(CHIPS):
                if (dz + g) % levels == 0:
                    sends[k].wait_recv()
            block = pl.ds(pl.multiple_of(core * half + lax.rem(zc + g, levels) * (2 * own), own), 2 * own)
            copy = pltpu.make_async_remote_copy(
                buf.at[block, span], buf.at[block, span], fs.at[row, j, g], fr.at[row, j, g],
                device_id=sibling, device_id_type=MESH,
            )
            copy.start()
            passed.append(copy)
        for copy in passed:
            copy.wait_recv()
        return passed + sends

    def permuted(weight, ordered):
        source = lax.broadcasted_iota(jnp.int32, (2 * half, 2 * half), 0)
        lane = lax.broadcasted_iota(jnp.int32, (1, 2 * half), 1)
        parity = jnp.where(lane < half, 0, 1)
        inner = lane - parity * half
        target = lax.div(inner, own) * (2 * own) + parity * own + lax.rem(inner, own)
        pick = jnp.where(source == target, 1.0, 0.0).astype(jnp.bfloat16)
        ordered[...] = jnp.dot(
            weight[...].reshape(taps * own, 2 * half), pick, preferred_element_type=jnp.float32
        ).astype(jnp.bfloat16)

    def halo(src, dst, sem, there):
        return pltpu.make_async_remote_copy(
            src, dst, hs.at[sem], hr.at[sem], device_id=(there, c), device_id_type=MESH
        )

    up, down = lax.rem(s + 1, ns), lax.rem(s + ns - 1, ns)

    def start_pair(pair):
        @pl.when(s < ns - 1)
        def _():
            pair[0].start()

        @pl.when(s > 0)
        def _():
            pair[1].start()

    def finish_pair(pair, low, high):
        @pl.when(s > 0)
        def _():
            pair[0].wait_recv()

        @pl.when(s == 0)
        def _():
            low[...] = jnp.zeros(low.shape, low.dtype)

        @pl.when(s < ns - 1)
        def _():
            pair[1].wait_recv()

        @pl.when(s == ns - 1)
        def _():
            high[...] = jnp.zeros(high.shape, high.dtype)

    def sent_pair(pair):
        @pl.when(s < ns - 1)
        def _():
            pair[0].wait_send()

        @pl.when(s > 0)
        def _():
            pair[1].wait_send()

    def fill(cols, field, a):
        plane = field[a + 1].astype(jnp.float32).reshape(rows, ny)
        for b in OFFSETS:
            side = moved(plane, b).astype(jnp.bfloat16)
            for e in OFFSETS:
                k = tap(a, b, e)
                for z in range(nz):
                    if 0 <= z + e < nz:
                        piece = side[(z + e) * own:(z + e + 1) * own]
                    else:
                        piece = jnp.zeros((own, ny), jnp.bfloat16)
                    cols[k * own:(k + 1) * own, z * ny:(z + 1) * ny] = piece

    def plane_sum(a, first, last):
        for z in range(first, last):
            total = None
            for b in OFFSETS:
                column = None
                for e in OFFSETS:
                    if 0 <= z - e < nz:
                        k = tap(a, b, e)
                        term = prod[k * own:(k + 1) * own, (z - e) * ny:(z - e + 1) * ny]
                        column = term if column is None else column + term
                column = moved(column, -b)
                total = column if total is None else total + column
            yield z, total

    def input_side(weight, got, row, j, ends_in, ends_out):
        span = lanes(j, ends_in)
        first, last = (ends_out[j - 1] if j else 0), ends_out[j]
        field = got[:, span]

        def product(a):
            lo = tap(a, -1, -1) * own
            left = weight[lo:lo + 9 * own, :]
            prod[lo:lo + 9 * own, span] = jnp.dot(left, field, preferred_element_type=jnp.float32)

        def copy(slot, there):
            part_z = pl.ds(first, last - first)
            return pltpu.make_async_remote_copy(
                send_q.at[row, slot, part_z], recv_q.at[row, slot, part_z], qs.at[row, j, slot], qr.at[row, j, slot],
                device_id=(there, c), device_id_type=MESH,
            )

        pair = copy(0, up), copy(1, down)
        for slot, a in ((0, 1), (1, -1)):
            product(a)
            for z, value in plane_sum(a, first, last):
                send_q[row, slot, z] = value.astype(jnp.bfloat16)

            @pl.when((s < ns - 1) if slot == 0 else (s > 0))
            def _():
                pair[slot].start()
        product(0)
        for z, value in plane_sum(0, first, last):
            center[z * own:(z + 1) * own, :] = value
        return pair

    def input_total(pair, row, j, ends):
        first, last = (ends[j - 1] if j else 0), ends[j]
        part_z = pl.ds(first, last - first)
        finish_pair(pair, recv_q.at[row, 0, part_z], recv_q.at[row, 1, part_z])
        low = recv_q[row, 0, first:last].astype(jnp.float32).reshape((last - first) * own, ny)
        high = recv_q[row, 1, first:last].astype(jnp.float32).reshape((last - first) * own, ny)
        return first, last, center[first * own:last * own, :] + low + high

    def weight_product(cols, got, span):
        value = lax.dot_general(
            got[:, span], cols[:, span], (((1,), (1,)), ((), ())), preferred_element_type=jnp.float32
        )
        return value.reshape(part.shape)

    def block_of(index):
        return pl.ds(pl.multiple_of(index * own, own), own)

    def weight_pack(row):
        send_part[row] = part[...].astype(jnp.bfloat16)
        return part[:, block_of(s), :]

    def weight_send(row):
        copies = []
        for d in DISTANCES:
            there = lax.rem(s + d, ns)
            block = block_of(there)
            copy = pltpu.make_async_remote_copy(
                send_part.at[row, :, block], recv_part.at[row, d - 1], ws.at[row, d - 1], wr.at[row, d - 1],
                device_id=(there, c), device_id_type=MESH,
            )
            copy.start()
            copies.append(copy)
        return copies

    side = lax.div(s, line)

    def near_send():
        copies = []
        for d in (2, 1, 3):
            place = lax.rem(s + d, line)
            for e in range(2):
                block = block_of(e * line + place)
                copies.append(pltpu.make_async_remote_copy(
                    send_part.at[0, :, block], near.at[d - 1, e], ns_sem.at[d - 1, e], nr_sem.at[d - 1, e],
                    device_id=(side * line + place, c), device_id_type=MESH,
                ))
        for copy in copies:
            copy.start()
        own_parts = [
            part[:, block_of(e * line + lax.rem(s, line)), :] for e in range(2)
        ]
        for e in range(2):
            line_sum[e] = own_parts[e]
        return copies

    def across_send(copies):
        for copy in copies:
            copy.wait_recv()
        for e in range(2):
            total = line_sum[e]
            for d in range(line - 1):
                total = total + near[d, e].astype(jnp.float32)
            line_sum[e] = total
            line_send[e] = total.astype(jnp.bfloat16)
        copy = pltpu.make_async_remote_copy(
            line_send.at[1 - side], opposite, os_sem, or_sem,
            device_id=((1 - side) * line + lax.rem(s, line), c), device_id_type=MESH,
        )
        copy.start()
        return copy

    def across_total(copy, ref):
        copy.wait_recv()
        total = line_sum[side] + opposite[...].astype(jnp.float32)
        ref[...] = (total.reshape(2 * own, -1)[:, :taps * own] * scale).T.reshape(ref.shape)

    def weight_total(total, copies, row, ref):
        for d, copy in zip(DISTANCES, copies):
            copy.wait_recv()
            total = total + recv_part[row, d - 1].astype(jnp.float32)
        ref[...] = (total.reshape(2 * own, -1)[:, :taps * own] * scale).T.reshape(ref.shape)

    chunks = len(ends_one)
    started = [start_gather(got_cot, 0, j, ends_one) for j in range(chunks)]

    loads[1].wait()
    value = pre[...].astype(jnp.float32).reshape(rows, ny)
    sig = jax.nn.sigmoid(value)
    hid[1] = (value * sig).astype(jnp.bfloat16).reshape(nz, own, ny)
    slope[...] = sig * (1.0 + value * (1.0 - sig))
    loads[2].wait()
    halo_copies = [
        (halo(hid.at[1], hid.at[0], 0, up), halo(hid.at[1], hid.at[2], 1, down)),
        (halo(layer.at[1], layer.at[0], 2, up), halo(layer.at[1], layer.at[2], 3, down)),
    ]
    for cols in (cols_two, cols_one):
        cols[taps * own:, :] = jnp.zeros((cols.shape[0] - taps * own, nz * ny), jnp.bfloat16)
    fill(cols_two, hid, 0)
    fill(cols_one, layer, 0)
    loads[3].wait()
    permuted(w2, ordered_two)
    loads[4].wait()
    permuted(w1, ordered_one)

    pending, pairs = [], []
    for j in range(chunks):
        pending += forward_gather(got_cot, 0, j, ends_one, started[j])
        pairs.append(input_side(ordered_two, got_cot, 0, j, ends_one, ends_two))
    start_pair(halo_copies[0])
    start_pair(halo_copies[1])
    started = []
    for j in range(chunks):
        first, last, grad = input_total(pairs[j], 0, j, ends_two)
        grad = (grad * slope[first * own:last * own, :]).astype(jnp.bfloat16)
        for z in range(first, last):
            got_pre[mine, z * ny:(z + 1) * ny] = grad[(z - first) * own:(z - first + 1) * own]
        started.append(start_gather(got_pre, 1, j, ends_two))
    finish_pair(halo_copies[0], hid.at[0], hid.at[2])
    fill(cols_two, hid, -1)
    fill(cols_two, hid, 1)
    part[...] = weight_product(cols_two, got_cot, pl.ds(0, nz * ny))
    weight_pack(0)
    near_copies = near_send()

    finish_pair(halo_copies[1], layer.at[0], layer.at[2])
    fill(cols_one, layer, -1)
    fill(cols_one, layer, 1)

    for j in range(chunks):
        pending += forward_gather(got_pre, 1, j, ends_two, started[j])
        piece = weight_product(cols_one, got_pre, lanes(j, ends_two))
        part[...] = piece if j == 0 else part[...] + piece
        if j == chunks - 1:
            total_one = weight_pack(1)
            copies_one = weight_send(1)
        pairs.append(input_side(ordered_one, got_pre, 1, j, ends_two, ends_three))
    across = across_send(near_copies)
    for copy in pending + near_copies:
        copy.wait_send()
    for pair in halo_copies + pairs[:chunks]:
        sent_pair(pair)
    for j in range(chunks):
        first, last, grad = input_total(pairs[chunks + j], 1, j, ends_three)
        out_ref[0, first:last] = grad.astype(jnp.bfloat16).reshape(last - first, own, ny)
    across_total(across, two_ref)
    for copy in [across] + copies_one:
        copy.wait_send()
    for pair in pairs[chunks:]:
        sent_pair(pair)
    weight_total(total_one, copies_one, 1, one_ref)


def hand_out(one_ref, two_ref, three_ref, one_out, two_out, three_out, sem):
    copies = [
        pltpu.make_async_copy(src, dst, sem.at[k])
        for k, (src, dst) in enumerate(((one_ref, one_out), (two_ref, two_out), (three_ref, three_out)))
    ]
    for copy in copies:
        copy.start()
    for copy in copies:
        copy.wait()


def solution(mesh):
    ns, groups = mesh.shape["space"], mesh.shape["chan"]

    def shards(layer_input, pre_act, out_grad, weight_one, weight_two):
        _, nz, own, ny = layer_input.shape
        taps, _, chans = weight_one.shape
        padded = -(-taps * own // 128) * 128
        scale = float(ns * ny * nz) ** -0.5
        chunks = 2
        ends = tuple(
            tuple(nz if j == chunks - 1 else nz * (j + 1) // chunks + shift for j in range(chunks)) for shift in (1, 0, -1)
        )
        any_space = pl.BlockSpec(memory_space=pl.ANY)
        vmem = pl.BlockSpec(memory_space=pltpu.VMEM)
        bf, f32 = jnp.bfloat16, jnp.float32
        dma = pltpu.SemaphoreType.DMA
        results = pl.pallas_call(
            functools.partial(kernel, (ns, nz, own, ny, scale, ends)),
            out_shape=(
                jax.ShapeDtypeStruct(layer_input.shape, bf),
                jax.ShapeDtypeStruct((taps, own, chans // ns), f32),
                jax.ShapeDtypeStruct((taps, own, chans // ns), f32),
            ),
            in_specs=[any_space] * 5,
            out_specs=(vmem, vmem, vmem),
            scratch_shapes=[
                pltpu.VMEM((3, nz, own, ny), bf),
                pltpu.VMEM((nz, own, ny), bf),
                pltpu.VMEM((nz, own, ny), bf),
                pltpu.VMEM(weight_one.shape, bf),
                pltpu.VMEM(weight_two.shape, bf),
                pltpu.VMEM((taps * own, chans), bf),
                pltpu.VMEM((taps * own, chans), bf),
                pltpu.VMEM((3, nz, own, ny), bf),
                pltpu.VMEM((nz * own, ny), f32),
                pltpu.VMEM((chans, nz * ny), bf),
                pltpu.VMEM((chans, nz * ny), bf),
                pltpu.VMEM((padded, nz * ny), bf),
                pltpu.VMEM((padded, nz * ny), bf),
                pltpu.VMEM((taps * own, nz * ny), f32),
                pltpu.VMEM((nz * own, ny), f32),
                pltpu.VMEM((2, chans // 2, padded), f32),
                pltpu.VMEM((2, 2, chans // 2, padded), bf),
                pltpu.VMEM((2, ns - 1, 2, own, padded), bf),
                pltpu.VMEM((ns // 2 - 1, 2, 2, own, padded), bf),
                pltpu.VMEM((2, 2, own, padded), f32),
                pltpu.VMEM((2, 2, own, padded), bf),
                pltpu.VMEM((2, own, padded), bf),
                pltpu.VMEM((2, 2, nz, own, ny), bf),
                pltpu.VMEM((2, 2, nz, own, ny), bf),
                dma((5,)),
                dma((2, chunks, len(CHIPS))),
                dma((2, chunks, len(CHIPS))),
                dma((2, chunks, len(GROUPS))),
                dma((2, chunks, len(GROUPS))),
                dma((4,)),
                dma((4,)),
                dma((2, chunks, 2)),
                dma((2, chunks, 2)),
                dma((2, ns - 1)),
                dma((2, ns - 1)),
                dma((ns // 2 - 1, 2)),
                dma((ns // 2 - 1, 2)),
                dma,
                dma,
            ],
            compiler_params=pltpu.CompilerParams(
                collective_id=0, has_side_effects=True, vmem_limit_bytes=48 * 1024 * 1024
            ),
        )(*[pltpu.with_memory_space_constraint(v, pltpu.HBM) for v in (layer_input, pre_act, out_grad, weight_one, weight_two)])
        return pl.pallas_call(
            hand_out,
            out_shape=tuple(jax.ShapeDtypeStruct(v.shape, v.dtype) for v in results),
            in_specs=[vmem] * 3,
            out_specs=(any_space,) * 3,
            scratch_shapes=[dma((3,))],
            compiler_params=pltpu.CompilerParams(vmem_limit_bytes=1024 * 1024),
        )(*results)

    wide, narrow = P("space", None, "chan", None), P(None, "chan", None)
    return jax.shard_map(
        shards,
        mesh=mesh,
        in_specs=(wide, wide, wide, narrow, narrow),
        out_specs=(wide, P(None, "chan", "space"), P(None, "chan", "space")),
        check_vma=False,
    )
```

```python
import functools

import jax
import jax.numpy as jnp
from jax import lax
from jax.experimental import pallas as pl
from jax.experimental.pallas import tpu as pltpu
from jax.sharding import PartitionSpec as P

MESH = pl.DeviceIdType.MESH
OFFSETS = (-1, 0, 1)
CHIPS = ((2, 2), (2, 0), (1, 2), (3, 2), (1, 0), (3, 0), (0, 2))


GROUPS = (0, 3, 1, 2)
DISTANCES = (2, 6, 1, 3, 5, 7, 4)


def tap(a, b, c):
    return 9 * (a + 1) + 3 * (b + 1) + (c + 1)


def moved(value, step):
    if step == 0:
        return value
    width = value.shape[1]
    lane = lax.broadcasted_iota(jnp.int32, value.shape, 1)
    inside = lane < width - step if step > 0 else lane >= -step
    return jnp.where(inside, pltpu.roll(value, (-step) % width, 1), 0.0)


def kernel(
    dims,
    layer_hbm, pre_hbm, cot_hbm, w1_hbm, w2_hbm,
    out_ref, one_ref, two_ref,
    layer, pre, cot, w1, w2, ordered_one, ordered_two, hid, slope,
    got_cot, got_pre, cols_one, cols_two, prod, center,
    part, send_part, recv_part, near, line_sum, line_send, opposite, send_q, recv_q,
    load_sem, gs, gr, fs, fr, hs, hr, qs, qr, ws, wr, ns_sem, nr_sem, os_sem, or_sem,
):
    ns, nz, own, ny, scale, (ends_one, ends_two, ends_three) = dims
    groups = got_cot.shape[0] // own
    rows = own * nz
    line = ns // 2
    taps = w1.shape[0]
    s = lax.axis_index("space")
    c = lax.axis_index("chan")
    zc, wc = lax.div(c, 4), lax.rem(c, 4)
    levels = groups // 4

    def chip(dz, dw):
        return lax.rem(zc + dz, levels) * 4 + (wc ^ dw)

    sibling = (s, c ^ 1)
    core, half = lax.rem(c, 2), got_cot.shape[0] // 2
    mine = pl.ds(pl.multiple_of(core * half + lax.div(c, 2) * own, own), own)

    barrier = pltpu.get_barrier_semaphore()
    partners = [(s, chip(*d)) for d in CHIPS] + [(lax.rem(s + d, ns), c) for d in range(1, ns)] + [sibling]
    for p in partners:
        pl.semaphore_signal(barrier, inc=1, device_id=p, device_id_type=MESH)

    loads = [
        pltpu.make_async_copy(src, dst, load_sem.at[k])
        for k, (src, dst) in enumerate(
            ((cot_hbm.at[0], cot), (pre_hbm.at[0], pre), (layer_hbm.at[0], layer.at[1]), (w2_hbm, w2), (w1_hbm, w1))
        )
    ]
    for copy in loads:
        copy.start()

    loads[0].wait()
    for z in range(nz):
        got_cot[mine, z * ny:(z + 1) * ny] = cot[z]
    pl.semaphore_wait(barrier, len(partners))

    def lanes(j, ends):
        start = ends[j - 1] if j else 0
        return pl.ds(start * ny, (ends[j] - start) * ny)

    def start_gather(buf, row, j, ends):
        span = lanes(j, ends)
        sends = []
        for k, d in enumerate(CHIPS):
            copy = pltpu.make_async_remote_copy(
                buf.at[mine, span], buf.at[mine, span], gs.at[row, j, k], gr.at[row, j, k],
                device_id=(s, chip(*d)), device_id_type=MESH,
            )
            copy.start()
            sends.append(copy)
        return sends

    def forward_gather(buf, row, j, ends, sends):
        span = lanes(j, ends)
        passed = []
        for g in GROUPS:
            for k, (dz, _) in enumerate(CHIPS):
                if (dz + g) % levels == 0:
                    sends[k].wait_recv()
            block = pl.ds(pl.multiple_of(core * half + lax.rem(zc + g, levels) * (2 * own), own), 2 * own)
            copy = pltpu.make_async_remote_copy(
                buf.at[block, span], buf.at[block, span], fs.at[row, j, g], fr.at[row, j, g],
                device_id=sibling, device_id_type=MESH,
            )
            copy.start()
            passed.append(copy)
        return passed, sends

    def permuted(weight, ordered):
        source = lax.broadcasted_iota(jnp.int32, (2 * half, 2 * half), 0)
        lane = lax.broadcasted_iota(jnp.int32, (1, 2 * half), 1)
        parity = jnp.where(lane < half, 0, 1)
        inner = lane - parity * half
        target = lax.div(inner, own) * (2 * own) + parity * own + lax.rem(inner, own)
        pick = jnp.where(source == target, 1.0, 0.0).astype(jnp.bfloat16)
        ordered[...] = jnp.dot(
            weight[...].reshape(taps * own, 2 * half), pick, preferred_element_type=jnp.float32
        ).astype(jnp.bfloat16)

    def halo(src, dst, sem, there):
        return pltpu.make_async_remote_copy(
            src, dst, hs.at[sem], hr.at[sem], device_id=(there, c), device_id_type=MESH
        )

    up, down = lax.rem(s + 1, ns), lax.rem(s + ns - 1, ns)

    def start_pair(pair):
        @pl.when(s < ns - 1)
        def _():
            pair[0].start()

        @pl.when(s > 0)
        def _():
            pair[1].start()

    def finish_pair(pair, low, high):
        @pl.when(s > 0)
        def _():
            pair[0].wait_recv()

        @pl.when(s == 0)
        def _():
            low[...] = jnp.zeros(low.shape, low.dtype)

        @pl.when(s < ns - 1)
        def _():
            pair[1].wait_recv()

        @pl.when(s == ns - 1)
        def _():
            high[...] = jnp.zeros(high.shape, high.dtype)

    def sent_pair(pair):
        @pl.when(s < ns - 1)
        def _():
            pair[0].wait_send()

        @pl.when(s > 0)
        def _():
            pair[1].wait_send()

    def fill(cols, field, a):
        plane = field[a + 1].astype(jnp.float32).reshape(rows, ny)
        for b in OFFSETS:
            side = moved(plane, b).astype(jnp.bfloat16)
            for e in OFFSETS:
                k = tap(a, b, e)
                for z in range(nz):
                    if 0 <= z + e < nz:
                        piece = side[(z + e) * own:(z + e + 1) * own]
                    else:
                        piece = jnp.zeros((own, ny), jnp.bfloat16)
                    cols[k * own:(k + 1) * own, z * ny:(z + 1) * ny] = piece

    def plane_sum(a, first, last):
        for z in range(first, last):
            total = None
            for b in OFFSETS:
                column = None
                for e in OFFSETS:
                    if 0 <= z - e < nz:
                        k = tap(a, b, e)
                        term = prod[k * own:(k + 1) * own, (z - e) * ny:(z - e + 1) * ny]
                        column = term if column is None else column + term
                column = moved(column, -b)
                total = column if total is None else total + column
            yield z, total

    def input_side(weight, got, row, j, ends_in, ends_out):
        span = lanes(j, ends_in)
        first, last = (ends_out[j - 1] if j else 0), ends_out[j]
        field = got[:, span]

        def product(a):
            lo = tap(a, -1, -1) * own
            left = weight[lo:lo + 9 * own, :]
            prod[lo:lo + 9 * own, span] = jnp.dot(left, field, preferred_element_type=jnp.float32)

        def copy(slot, there):
            part_z = pl.ds(first, last - first)
            return pltpu.make_async_remote_copy(
                send_q.at[row, slot, part_z], recv_q.at[row, slot, part_z], qs.at[row, j, slot], qr.at[row, j, slot],
                device_id=(there, c), device_id_type=MESH,
            )

        pair = copy(0, up), copy(1, down)
        for slot, a in ((0, 1), (1, -1)):
            product(a)
            for z, value in plane_sum(a, first, last):
                send_q[row, slot, z] = value.astype(jnp.bfloat16)

            @pl.when((s < ns - 1) if slot == 0 else (s > 0))
            def _():
                pair[slot].start()
        product(0)
        for z, value in plane_sum(0, first, last):
            center[z * own:(z + 1) * own, :] = value
        return pair

    def input_total(pair, row, j, ends):
        first, last = (ends[j - 1] if j else 0), ends[j]
        part_z = pl.ds(first, last - first)
        finish_pair(pair, recv_q.at[row, 0, part_z], recv_q.at[row, 1, part_z])
        low = recv_q[row, 0, first:last].astype(jnp.float32).reshape((last - first) * own, ny)
        high = recv_q[row, 1, first:last].astype(jnp.float32).reshape((last - first) * own, ny)
        return first, last, center[first * own:last * own, :] + low + high

    def weight_product(cols, got, span):
        value = lax.dot_general(
            got[:, span], cols[:, span], (((1,), (1,)), ((), ())), preferred_element_type=jnp.float32
        )
        return value.reshape(part.shape)

    def block_of(index):
        return pl.ds(pl.multiple_of(index * own, own), own)

    def weight_half(parity, span, add):
        strip = pl.ds(pl.multiple_of(parity * half, half), half)
        piece = lax.dot_general(
            got_pre[strip, span], cols_one[:, span], (((1,), (1,)), ((), ())), preferred_element_type=jnp.float32
        )
        part[parity] = part[parity] + piece if add else piece

    def half_send(turn, parity):
        send_part[1, parity] = part[parity].astype(jnp.bfloat16)
        copies = []
        for d in DISTANCES:
            there = lax.rem(s + d, ns)
            copy = pltpu.make_async_remote_copy(
                send_part.at[1, parity, block_of(there)], recv_part.at[d - 1, parity],
                ws.at[turn, d - 1], wr.at[turn, d - 1], device_id=(there, c), device_id_type=MESH,
            )
            copy.start()
            copies.append(copy)
        return copies

    side = lax.div(s, line)

    def near_send():
        copies = []
        for d in (2, 1, 3):
            place = lax.rem(s + d, line)
            for e in range(2):
                block = block_of(e * line + place)
                copies.append(pltpu.make_async_remote_copy(
                    send_part.at[0, :, block], near.at[d - 1, e], ns_sem.at[d - 1, e], nr_sem.at[d - 1, e],
                    device_id=(side * line + place, c), device_id_type=MESH,
                ))
        for copy in copies:
            copy.start()
        own_parts = [
            part[:, block_of(e * line + lax.rem(s, line)), :] for e in range(2)
        ]
        for e in range(2):
            line_sum[e] = own_parts[e]
        return copies

    def across_send(copies):
        for copy in copies:
            copy.wait_recv()
        for e in range(2):
            total = line_sum[e]
            for d in range(line - 1):
                total = total + near[d, e].astype(jnp.float32)
            line_sum[e] = total
            line_send[e] = total.astype(jnp.bfloat16)
        copy = pltpu.make_async_remote_copy(
            line_send.at[1 - side], opposite, os_sem, or_sem,
            device_id=((1 - side) * line + lax.rem(s, line), c), device_id_type=MESH,
        )
        copy.start()
        return copy

    def across_total(copy, ref):
        copy.wait_recv()
        total = line_sum[side] + opposite[...].astype(jnp.float32)
        ref[...] = (total.reshape(2 * own, -1)[:, :taps * own] * scale).T.reshape(ref.shape)

    def weight_total(copies, ref):
        for copy in copies:
            copy.wait_recv()
        total = part[:, block_of(s), :]
        for d in range(ns - 1):
            total = total + recv_part[d].astype(jnp.float32)
        ref[...] = (total.reshape(2 * own, -1)[:, :taps * own] * scale).T.reshape(ref.shape)

    chunks = len(ends_one)
    started = [start_gather(got_cot, 0, j, ends_one) for j in range(chunks)]

    loads[1].wait()
    value = pre[...].astype(jnp.float32).reshape(rows, ny)
    sig = jax.nn.sigmoid(value)
    hid[1] = (value * sig).astype(jnp.bfloat16).reshape(nz, own, ny)
    slope[...] = sig * (1.0 + value * (1.0 - sig))
    loads[2].wait()
    halo_copies = [
        (halo(hid.at[1], hid.at[0], 0, up), halo(hid.at[1], hid.at[2], 1, down)),
        (halo(layer.at[1], layer.at[0], 2, up), halo(layer.at[1], layer.at[2], 3, down)),
    ]
    for cols in (cols_two, cols_one):
        cols[taps * own:, :] = jnp.zeros((cols.shape[0] - taps * own, nz * ny), jnp.bfloat16)
    fill(cols_two, hid, 0)
    fill(cols_one, layer, 0)
    loads[3].wait()
    permuted(w2, ordered_two)
    loads[4].wait()
    permuted(w1, ordered_one)

    pending, pairs = [], []
    for j in range(chunks):
        passed, sends = forward_gather(got_cot, 0, j, ends_one, started[j])
        for copy in passed:
            copy.wait_recv()
        pending += passed + sends
        pairs.append(input_side(ordered_two, got_cot, 0, j, ends_one, ends_two))
    start_pair(halo_copies[0])
    start_pair(halo_copies[1])
    started = []
    for j in range(chunks):
        first, last, grad = input_total(pairs[j], 0, j, ends_two)
        grad = (grad * slope[first * own:last * own, :]).astype(jnp.bfloat16)
        for z in range(first, last):
            got_pre[mine, z * ny:(z + 1) * ny] = grad[(z - first) * own:(z - first + 1) * own]
        started.append(start_gather(got_pre, 1, j, ends_two))
    finish_pair(halo_copies[0], hid.at[0], hid.at[2])
    fill(cols_two, hid, -1)
    fill(cols_two, hid, 1)
    part[...] = weight_product(cols_two, got_cot, pl.ds(0, nz * ny))
    send_part[0] = part[...].astype(jnp.bfloat16)
    near_copies = near_send()

    finish_pair(halo_copies[1], layer.at[0], layer.at[2])
    fill(cols_one, layer, -1)
    fill(cols_one, layer, 1)

    copies_one = []
    for j in range(chunks):
        passed, sends = forward_gather(got_pre, 1, j, ends_two, started[j])
        for turn, parity in enumerate((core, 1 - core)):
            if turn:
                for copy in passed:
                    copy.wait_recv()
            weight_half(parity, lanes(j, ends_two), j > 0)
            if j == chunks - 1:
                copies_one += half_send(turn, parity)
        pending += passed + sends
        pairs.append(input_side(ordered_one, got_pre, 1, j, ends_two, ends_three))
    across = across_send(near_copies)
    for copy in pending + near_copies:
        copy.wait_send()
    for pair in halo_copies + pairs[:chunks]:
        sent_pair(pair)
    for j in range(chunks):
        first, last, grad = input_total(pairs[chunks + j], 1, j, ends_three)
        out_ref[0, first:last] = grad.astype(jnp.bfloat16).reshape(last - first, own, ny)
    across_total(across, two_ref)
    for copy in [across] + copies_one:
        copy.wait_send()
    for pair in pairs[chunks:]:
        sent_pair(pair)
    weight_total(copies_one, one_ref)


def hand_out(one_ref, two_ref, three_ref, one_out, two_out, three_out, sem):
    copies = [
        pltpu.make_async_copy(src, dst, sem.at[k])
        for k, (src, dst) in enumerate(((one_ref, one_out), (two_ref, two_out), (three_ref, three_out)))
    ]
    for copy in copies:
        copy.start()
    for copy in copies:
        copy.wait()


def solution(mesh):
    ns, groups = mesh.shape["space"], mesh.shape["chan"]

    def shards(layer_input, pre_act, out_grad, weight_one, weight_two):
        _, nz, own, ny = layer_input.shape
        taps, _, chans = weight_one.shape
        padded = -(-taps * own // 128) * 128
        scale = float(ns * ny * nz) ** -0.5
        chunks = 2
        ends = tuple(
            tuple(nz if j == chunks - 1 else nz * (j + 1) // chunks + shift for j in range(chunks)) for shift in (1, 0, -1)
        )
        any_space = pl.BlockSpec(memory_space=pl.ANY)
        vmem = pl.BlockSpec(memory_space=pltpu.VMEM)
        bf, f32 = jnp.bfloat16, jnp.float32
        dma = pltpu.SemaphoreType.DMA
        results = pl.pallas_call(
            functools.partial(kernel, (ns, nz, own, ny, scale, ends)),
            out_shape=(
                jax.ShapeDtypeStruct(layer_input.shape, bf),
                jax.ShapeDtypeStruct((taps, own, chans // ns), f32),
                jax.ShapeDtypeStruct((taps, own, chans // ns), f32),
            ),
            in_specs=[any_space] * 5,
            out_specs=(vmem, vmem, vmem),
            scratch_shapes=[
                pltpu.VMEM((3, nz, own, ny), bf),
                pltpu.VMEM((nz, own, ny), bf),
                pltpu.VMEM((nz, own, ny), bf),
                pltpu.VMEM(weight_one.shape, bf),
                pltpu.VMEM(weight_two.shape, bf),
                pltpu.VMEM((taps * own, chans), bf),
                pltpu.VMEM((taps * own, chans), bf),
                pltpu.VMEM((3, nz, own, ny), bf),
                pltpu.VMEM((nz * own, ny), f32),
                pltpu.VMEM((chans, nz * ny), bf),
                pltpu.VMEM((chans, nz * ny), bf),
                pltpu.VMEM((padded, nz * ny), bf),
                pltpu.VMEM((padded, nz * ny), bf),
                pltpu.VMEM((taps * own, nz * ny), f32),
                pltpu.VMEM((nz * own, ny), f32),
                pltpu.VMEM((2, chans // 2, padded), f32),
                pltpu.VMEM((2, 2, chans // 2, padded), bf),
                pltpu.VMEM((ns - 1, 2, own, padded), bf),
                pltpu.VMEM((ns // 2 - 1, 2, 2, own, padded), bf),
                pltpu.VMEM((2, 2, own, padded), f32),
                pltpu.VMEM((2, 2, own, padded), bf),
                pltpu.VMEM((2, own, padded), bf),
                pltpu.VMEM((2, 2, nz, own, ny), bf),
                pltpu.VMEM((2, 2, nz, own, ny), bf),
                dma((5,)),
                dma((2, chunks, len(CHIPS))),
                dma((2, chunks, len(CHIPS))),
                dma((2, chunks, len(GROUPS))),
                dma((2, chunks, len(GROUPS))),
                dma((4,)),
                dma((4,)),
                dma((2, chunks, 2)),
                dma((2, chunks, 2)),
                dma((2, ns - 1)),
                dma((2, ns - 1)),
                dma((ns // 2 - 1, 2)),
                dma((ns // 2 - 1, 2)),
                dma,
                dma,
            ],
            compiler_params=pltpu.CompilerParams(
                collective_id=0, has_side_effects=True, vmem_limit_bytes=48 * 1024 * 1024
            ),
        )(*[pltpu.with_memory_space_constraint(v, pltpu.HBM) for v in (layer_input, pre_act, out_grad, weight_one, weight_two)])
        return pl.pallas_call(
            hand_out,
            out_shape=tuple(jax.ShapeDtypeStruct(v.shape, v.dtype) for v in results),
            in_specs=[vmem] * 3,
            out_specs=(any_space,) * 3,
            scratch_shapes=[dma((3,))],
            compiler_params=pltpu.CompilerParams(vmem_limit_bytes=1024 * 1024),
        )(*results)

    wide, narrow = P("space", None, "chan", None), P(None, "chan", None)
    return jax.shard_map(
        shards,
        mesh=mesh,
        in_specs=(wide, wide, wide, narrow, narrow),
        out_specs=(wide, P(None, "chan", "space"), P(None, "chan", "space")),
        check_vma=False,
    )
```

```python
import functools

import jax
import jax.numpy as jnp
from jax import lax
from jax.experimental import pallas as pl
from jax.experimental.pallas import tpu as pltpu
from jax.sharding import PartitionSpec as P

MESH = pl.DeviceIdType.MESH
OFFSETS = (-1, 0, 1)
CHIPS = ((2, 2), (2, 0), (1, 2), (3, 2), (1, 0), (3, 0), (0, 2))


GROUPS = (0, 3, 1, 2)
DISTANCES = (2, 6, 1, 3, 5, 7, 4)


def tap(a, b, c):
    return 9 * (a + 1) + 3 * (b + 1) + (c + 1)


def moved(value, step):
    if step == 0:
        return value
    width = value.shape[1]
    lane = lax.broadcasted_iota(jnp.int32, value.shape, 1)
    inside = lane < width - step if step > 0 else lane >= -step
    return jnp.where(inside, pltpu.roll(value, (-step) % width, 1), 0.0)


def kernel(
    dims,
    layer_hbm, pre_hbm, cot_hbm, w1_hbm, w2_hbm,
    out_ref, one_ref, two_ref,
    layer, pre, cot, w1, w2, ordered_one, ordered_two, hid, slope,
    got_cot, got_pre, cols_one, cols_two, prod, center,
    part, send_part, recv_part, near, line_sum, line_send, opposite, send_q, recv_q,
    load_sem, gs, gr, fs, fr, hs, hr, qs, qr, ws, wr, ns_sem, nr_sem, os_sem, or_sem,
):
    ns, nz, own, ny, scale, (ends_one, ends_two, ends_three) = dims
    groups = got_cot.shape[0] // own
    rows = own * nz
    line = ns // 2
    taps = w1.shape[0]
    s = lax.axis_index("space")
    c = lax.axis_index("chan")
    zc, wc = lax.div(c, 4), lax.rem(c, 4)
    levels = groups // 4

    def chip(dz, dw):
        return lax.rem(zc + dz, levels) * 4 + (wc ^ dw)

    sibling = (s, c ^ 1)
    core, half = lax.rem(c, 2), got_cot.shape[0] // 2
    mine = pl.ds(pl.multiple_of(core * half + lax.div(c, 2) * own, own), own)

    barrier = pltpu.get_barrier_semaphore()
    partners = [(s, chip(*d)) for d in CHIPS] + [(lax.rem(s + d, ns), c) for d in range(1, ns)] + [sibling]
    for p in partners:
        pl.semaphore_signal(barrier, inc=1, device_id=p, device_id_type=MESH)

    loads = [
        pltpu.make_async_copy(src, dst, load_sem.at[k])
        for k, (src, dst) in enumerate(
            ((cot_hbm.at[0], cot), (pre_hbm.at[0], pre), (layer_hbm.at[0], layer.at[1]), (w2_hbm, w2), (w1_hbm, w1))
        )
    ]
    for copy in loads:
        copy.start()

    loads[0].wait()
    for z in range(nz):
        got_cot[mine, z * ny:(z + 1) * ny] = cot[z]
    pl.semaphore_wait(barrier, len(partners))

    def lanes(j, ends):
        start = ends[j - 1] if j else 0
        return pl.ds(start * ny, (ends[j] - start) * ny)

    def start_gather(buf, row, j, ends):
        span = lanes(j, ends)
        sends = []
        for k, d in enumerate(CHIPS):
            copy = pltpu.make_async_remote_copy(
                buf.at[mine, span], buf.at[mine, span], gs.at[row, j, k], gr.at[row, j, k],
                device_id=(s, chip(*d)), device_id_type=MESH,
            )
            copy.start()
            sends.append(copy)
        return sends

    def forward_gather(buf, row, j, ends, sends):
        span = lanes(j, ends)
        passed = []
        for g in GROUPS:
            for k, (dz, _) in enumerate(CHIPS):
                if (dz + g) % levels == 0:
                    sends[k].wait_recv()
            block = pl.ds(pl.multiple_of(core * half + lax.rem(zc + g, levels) * (2 * own), own), 2 * own)
            copy = pltpu.make_async_remote_copy(
                buf.at[block, span], buf.at[block, span], fs.at[row, j, g], fr.at[row, j, g],
                device_id=sibling, device_id_type=MESH,
            )
            copy.start()
            passed.append(copy)
        return passed, sends

    def permuted(weight, ordered):
        source = lax.broadcasted_iota(jnp.int32, (2 * half, 2 * half), 0)
        lane = lax.broadcasted_iota(jnp.int32, (1, 2 * half), 1)
        parity = jnp.where(lane < half, 0, 1)
        inner = lane - parity * half
        target = lax.div(inner, own) * (2 * own) + parity * own + lax.rem(inner, own)
        pick = jnp.where(source == target, 1.0, 0.0).astype(jnp.bfloat16)
        ordered[...] = jnp.dot(
            weight[...].reshape(taps * own, 2 * half), pick, preferred_element_type=jnp.float32
        ).astype(jnp.bfloat16)

    def halo(src, dst, sem, there):
        return pltpu.make_async_remote_copy(
            src, dst, hs.at[sem], hr.at[sem], device_id=(there, c), device_id_type=MESH
        )

    up, down = lax.rem(s + 1, ns), lax.rem(s + ns - 1, ns)

    def start_pair(pair):
        @pl.when(s < ns - 1)
        def _():
            pair[0].start()

        @pl.when(s > 0)
        def _():
            pair[1].start()

    def finish_pair(pair, low, high):
        @pl.when(s > 0)
        def _():
            pair[0].wait_recv()

        @pl.when(s == 0)
        def _():
            low[...] = jnp.zeros(low.shape, low.dtype)

        @pl.when(s < ns - 1)
        def _():
            pair[1].wait_recv()

        @pl.when(s == ns - 1)
        def _():
            high[...] = jnp.zeros(high.shape, high.dtype)

    def sent_pair(pair):
        @pl.when(s < ns - 1)
        def _():
            pair[0].wait_send()

        @pl.when(s > 0)
        def _():
            pair[1].wait_send()

    def fill(cols, field, a):
        plane = field[a + 1].astype(jnp.float32).reshape(rows, ny)
        for b in OFFSETS:
            side = moved(plane, b).astype(jnp.bfloat16)
            for e in OFFSETS:
                k = tap(a, b, e)
                for z in range(nz):
                    if 0 <= z + e < nz:
                        piece = side[(z + e) * own:(z + e + 1) * own]
                    else:
                        piece = jnp.zeros((own, ny), jnp.bfloat16)
                    cols[k * own:(k + 1) * own, z * ny:(z + 1) * ny] = piece

    def plane_sum(a, first, last):
        for z in range(first, last):
            total = None
            for b in OFFSETS:
                column = None
                for e in OFFSETS:
                    if 0 <= z - e < nz:
                        k = tap(a, b, e)
                        term = prod[k * own:(k + 1) * own, (z - e) * ny:(z - e + 1) * ny]
                        column = term if column is None else column + term
                column = moved(column, -b)
                total = column if total is None else total + column
            yield z, total

    def input_side(weight, got, row, j, ends_in, ends_out):
        span = lanes(j, ends_in)
        first, last = (ends_out[j - 1] if j else 0), ends_out[j]
        field = got[:, span]

        def product(a):
            lo = tap(a, -1, -1) * own
            left = weight[lo:lo + 9 * own, :]
            prod[lo:lo + 9 * own, span] = jnp.dot(left, field, preferred_element_type=jnp.float32)

        def copy(slot, there):
            part_z = pl.ds(first, last - first)
            return pltpu.make_async_remote_copy(
                send_q.at[row, slot, part_z], recv_q.at[row, slot, part_z], qs.at[row, j, slot], qr.at[row, j, slot],
                device_id=(there, c), device_id_type=MESH,
            )

        pair = copy(0, up), copy(1, down)
        for slot, a in ((0, 1), (1, -1)):
            product(a)
            for z, value in plane_sum(a, first, last):
                send_q[row, slot, z] = value.astype(jnp.bfloat16)

            @pl.when((s < ns - 1) if slot == 0 else (s > 0))
            def _():
                pair[slot].start()
        product(0)
        for z, value in plane_sum(0, first, last):
            center[z * own:(z + 1) * own, :] = value
        return pair

    def input_total(pair, row, j, ends):
        first, last = (ends[j - 1] if j else 0), ends[j]
        part_z = pl.ds(first, last - first)
        finish_pair(pair, recv_q.at[row, 0, part_z], recv_q.at[row, 1, part_z])
        low = recv_q[row, 0, first:last].astype(jnp.float32).reshape((last - first) * own, ny)
        high = recv_q[row, 1, first:last].astype(jnp.float32).reshape((last - first) * own, ny)
        return first, last, center[first * own:last * own, :] + low + high

    def weight_product(cols, got, span):
        value = lax.dot_general(
            got[:, span], cols[:, span], (((1,), (1,)), ((), ())), preferred_element_type=jnp.float32
        )
        return value.reshape(part.shape)

    def block_of(index):
        return pl.ds(pl.multiple_of(index * own, own), own)

    def weight_half(parity, span, add):
        strip = pl.ds(pl.multiple_of(parity * half, half), half)
        piece = lax.dot_general(
            got_pre[strip, span], cols_one[:, span], (((1,), (1,)), ((), ())), preferred_element_type=jnp.float32
        )
        part[parity] = part[parity] + piece if add else piece

    def half_send(turn, parity):
        send_part[1, parity] = part[parity].astype(jnp.bfloat16)
        copies = []
        for d in DISTANCES:
            there = lax.rem(s + d, ns)
            copy = pltpu.make_async_remote_copy(
                send_part.at[1, parity, block_of(there)], recv_part.at[d - 1, parity],
                ws.at[turn, d - 1], wr.at[turn, d - 1], device_id=(there, c), device_id_type=MESH,
            )
            copy.start()
            copies.append(copy)
        return copies

    side = lax.div(s, line)

    def near_send():
        copies = []
        for d in (2, 1, 3):
            place = lax.rem(s + d, line)
            for e in range(2):
                block = block_of(e * line + place)
                copies.append(pltpu.make_async_remote_copy(
                    send_part.at[0, :, block], near.at[d - 1, e], ns_sem.at[d - 1, e], nr_sem.at[d - 1, e],
                    device_id=(side * line + place, c), device_id_type=MESH,
                ))
        for copy in copies:
            copy.start()
        own_parts = [
            part[:, block_of(e * line + lax.rem(s, line)), :] for e in range(2)
        ]
        for e in range(2):
            line_sum[e] = own_parts[e]
        return copies

    def across_send(copies):
        for copy in copies:
            copy.wait_recv()
        for e in range(2):
            total = line_sum[e]
            for d in range(line - 1):
                total = total + near[d, e].astype(jnp.float32)
            line_sum[e] = total
            line_send[e] = total.astype(jnp.bfloat16)
        copy = pltpu.make_async_remote_copy(
            line_send.at[1 - side], opposite, os_sem, or_sem,
            device_id=((1 - side) * line + lax.rem(s, line), c), device_id_type=MESH,
        )
        copy.start()
        return copy

    def across_total(copy, ref):
        copy.wait_recv()
        total = line_sum[side] + opposite[...].astype(jnp.float32)
        ref[...] = (total.reshape(2 * own, -1)[:, :taps * own] * scale).T.reshape(ref.shape)

    def weight_total(copies, ref):
        for copy in copies:
            copy.wait_recv()
        total = part[:, block_of(s), :]
        for d in range(ns - 1):
            total = total + recv_part[d].astype(jnp.float32)
        ref[...] = (total.reshape(2 * own, -1)[:, :taps * own] * scale).T.reshape(ref.shape)

    chunks = len(ends_one)
    started = [start_gather(got_cot, 0, j, ends_one) for j in range(chunks)]

    loads[1].wait()
    value = pre[...].astype(jnp.float32).reshape(rows, ny)
    sig = jax.nn.sigmoid(value)
    hid[1] = (value * sig).astype(jnp.bfloat16).reshape(nz, own, ny)
    slope[...] = sig * (1.0 + value * (1.0 - sig))
    loads[2].wait()
    halo_copies = [
        (halo(hid.at[1], hid.at[0], 0, up), halo(hid.at[1], hid.at[2], 1, down)),
        (halo(layer.at[1], layer.at[0], 2, up), halo(layer.at[1], layer.at[2], 3, down)),
    ]
    for cols in (cols_two, cols_one):
        cols[taps * own:, :] = jnp.zeros((cols.shape[0] - taps * own, nz * ny), jnp.bfloat16)
    fill(cols_two, hid, 0)
    fill(cols_one, layer, 0)
    loads[3].wait()
    permuted(w2, ordered_two)
    loads[4].wait()
    permuted(w1, ordered_one)

    pending, pairs = [], []
    for j in range(chunks):
        passed, sends = forward_gather(got_cot, 0, j, ends_one, started[j])
        for copy in passed:
            copy.wait_recv()
        pending += passed + sends
        pairs.append(input_side(ordered_two, got_cot, 0, j, ends_one, ends_two))
        if j == 0:
            start_pair(halo_copies[0])
    start_pair(halo_copies[1])
    started = []
    for j in range(chunks):
        first, last, grad = input_total(pairs[j], 0, j, ends_two)
        grad = (grad * slope[first * own:last * own, :]).astype(jnp.bfloat16)
        for z in range(first, last):
            got_pre[mine, z * ny:(z + 1) * ny] = grad[(z - first) * own:(z - first + 1) * own]
        started.append(start_gather(got_pre, 1, j, ends_two))
    finish_pair(halo_copies[0], hid.at[0], hid.at[2])
    fill(cols_two, hid, -1)
    fill(cols_two, hid, 1)
    part[...] = weight_product(cols_two, got_cot, pl.ds(0, nz * ny))
    send_part[0] = part[...].astype(jnp.bfloat16)
    near_copies = near_send()

    finish_pair(halo_copies[1], layer.at[0], layer.at[2])
    fill(cols_one, layer, -1)
    fill(cols_one, layer, 1)

    copies_one = []
    for j in range(chunks):
        passed, sends = forward_gather(got_pre, 1, j, ends_two, started[j])
        for turn, parity in enumerate((core, 1 - core)):
            if turn:
                for copy in passed:
                    copy.wait_recv()
            weight_half(parity, lanes(j, ends_two), j > 0)
            if j == chunks - 1:
                copies_one += half_send(turn, parity)
        pending += passed + sends
        pairs.append(input_side(ordered_one, got_pre, 1, j, ends_two, ends_three))
    across = across_send(near_copies)
    for copy in pending + near_copies:
        copy.wait_send()
    for pair in halo_copies + pairs[:chunks]:
        sent_pair(pair)
    for j in range(chunks):
        first, last, grad = input_total(pairs[chunks + j], 1, j, ends_three)
        out_ref[0, first:last] = grad.astype(jnp.bfloat16).reshape(last - first, own, ny)
    across_total(across, two_ref)
    for copy in [across] + copies_one:
        copy.wait_send()
    for pair in pairs[chunks:]:
        sent_pair(pair)
    weight_total(copies_one, one_ref)


def hand_out(one_ref, two_ref, three_ref, one_out, two_out, three_out, sem):
    copies = [
        pltpu.make_async_copy(src, dst, sem.at[k])
        for k, (src, dst) in enumerate(((one_ref, one_out), (two_ref, two_out), (three_ref, three_out)))
    ]
    for copy in copies:
        copy.start()
    for copy in copies:
        copy.wait()


def solution(mesh):
    ns, groups = mesh.shape["space"], mesh.shape["chan"]

    def shards(layer_input, pre_act, out_grad, weight_one, weight_two):
        _, nz, own, ny = layer_input.shape
        taps, _, chans = weight_one.shape
        padded = -(-taps * own // 128) * 128
        scale = float(ns * ny * nz) ** -0.5
        chunks = 2
        ends = tuple(
            tuple(nz if j == chunks - 1 else nz * (j + 1) // chunks + shift for j in range(chunks)) for shift in (1, 0, -1)
        )
        any_space = pl.BlockSpec(memory_space=pl.ANY)
        vmem = pl.BlockSpec(memory_space=pltpu.VMEM)
        bf, f32 = jnp.bfloat16, jnp.float32
        dma = pltpu.SemaphoreType.DMA
        results = pl.pallas_call(
            functools.partial(kernel, (ns, nz, own, ny, scale, ends)),
            out_shape=(
                jax.ShapeDtypeStruct(layer_input.shape, bf),
                jax.ShapeDtypeStruct((taps, own, chans // ns), f32),
                jax.ShapeDtypeStruct((taps, own, chans // ns), f32),
            ),
            in_specs=[any_space] * 5,
            out_specs=(vmem, vmem, vmem),
            scratch_shapes=[
                pltpu.VMEM((3, nz, own, ny), bf),
                pltpu.VMEM((nz, own, ny), bf),
                pltpu.VMEM((nz, own, ny), bf),
                pltpu.VMEM(weight_one.shape, bf),
                pltpu.VMEM(weight_two.shape, bf),
                pltpu.VMEM((taps * own, chans), bf),
                pltpu.VMEM((taps * own, chans), bf),
                pltpu.VMEM((3, nz, own, ny), bf),
                pltpu.VMEM((nz * own, ny), f32),
                pltpu.VMEM((chans, nz * ny), bf),
                pltpu.VMEM((chans, nz * ny), bf),
                pltpu.VMEM((padded, nz * ny), bf),
                pltpu.VMEM((padded, nz * ny), bf),
                pltpu.VMEM((taps * own, nz * ny), f32),
                pltpu.VMEM((nz * own, ny), f32),
                pltpu.VMEM((2, chans // 2, padded), f32),
                pltpu.VMEM((2, 2, chans // 2, padded), bf),
                pltpu.VMEM((ns - 1, 2, own, padded), bf),
                pltpu.VMEM((ns // 2 - 1, 2, 2, own, padded), bf),
                pltpu.VMEM((2, 2, own, padded), f32),
                pltpu.VMEM((2, 2, own, padded), bf),
                pltpu.VMEM((2, own, padded), bf),
                pltpu.VMEM((2, 2, nz, own, ny), bf),
                pltpu.VMEM((2, 2, nz, own, ny), bf),
                dma((5,)),
                dma((2, chunks, len(CHIPS))),
                dma((2, chunks, len(CHIPS))),
                dma((2, chunks, len(GROUPS))),
                dma((2, chunks, len(GROUPS))),
                dma((4,)),
                dma((4,)),
                dma((2, chunks, 2)),
                dma((2, chunks, 2)),
                dma((2, ns - 1)),
                dma((2, ns - 1)),
                dma((ns // 2 - 1, 2)),
                dma((ns // 2 - 1, 2)),
                dma,
                dma,
            ],
            compiler_params=pltpu.CompilerParams(
                collective_id=0, has_side_effects=True, vmem_limit_bytes=48 * 1024 * 1024
            ),
        )(*[pltpu.with_memory_space_constraint(v, pltpu.HBM) for v in (layer_input, pre_act, out_grad, weight_one, weight_two)])
        return pl.pallas_call(
            hand_out,
            out_shape=tuple(jax.ShapeDtypeStruct(v.shape, v.dtype) for v in results),
            in_specs=[vmem] * 3,
            out_specs=(any_space,) * 3,
            scratch_shapes=[dma((3,))],
            compiler_params=pltpu.CompilerParams(vmem_limit_bytes=1024 * 1024),
        )(*results)

    wide, narrow = P("space", None, "chan", None), P(None, "chan", None)
    return jax.shard_map(
        shards,
        mesh=mesh,
        in_specs=(wide, wide, wide, narrow, narrow),
        out_specs=(wide, P(None, "chan", "space"), P(None, "chan", "space")),
        check_vma=False,
    )
```

```python
import functools

import jax
import jax.numpy as jnp
from jax import lax
from jax.experimental import pallas as pl
from jax.experimental.pallas import tpu as pltpu
from jax.sharding import PartitionSpec as P

MESH = pl.DeviceIdType.MESH
OFFSETS = (-1, 0, 1)
CHIPS = ((2, 2), (2, 0), (1, 2), (3, 2), (1, 0), (3, 0), (0, 2))


GROUPS = (0, 3, 1, 2)
DISTANCES = (2, 6, 1, 3, 5, 7, 4)


def tap(a, b, c):
    return 9 * (a + 1) + 3 * (b + 1) + (c + 1)


def moved(value, step):
    if step == 0:
        return value
    width = value.shape[1]
    lane = lax.broadcasted_iota(jnp.int32, value.shape, 1)
    inside = lane < width - step if step > 0 else lane >= -step
    return jnp.where(inside, pltpu.roll(value, (-step) % width, 1), 0.0)


def kernel(
    dims,
    layer_hbm, pre_hbm, cot_hbm, w1_hbm, w2_hbm,
    out_ref, one_ref, two_ref,
    layer, pre, cot, w1, w2, ordered_one, ordered_two, hid, slope,
    got_cot, got_pre, cols_one, cols_two, prod, center,
    part, send_part, recv_part, near, line_sum, line_send, opposite, send_q, recv_q,
    load_sem, gs, gr, fs, fr, hs, hr, qs, qr, ws, wr, ns_sem, nr_sem, os_sem, or_sem,
):
    ns, nz, own, ny, scale, (ends_one, ends_two, ends_three) = dims
    groups = got_cot.shape[0] // own
    rows = own * nz
    line = ns // 2
    taps = w1.shape[0]
    s = lax.axis_index("space")
    c = lax.axis_index("chan")
    zc, wc = lax.div(c, 4), lax.rem(c, 4)
    levels = groups // 4

    def chip(dz, dw):
        return lax.rem(zc + dz, levels) * 4 + (wc ^ dw)

    sibling = (s, c ^ 1)
    core, half = lax.rem(c, 2), got_cot.shape[0] // 2
    mine = pl.ds(pl.multiple_of(core * half + lax.div(c, 2) * own, own), own)

    barrier = pltpu.get_barrier_semaphore()
    partners = [(s, chip(*d)) for d in CHIPS] + [(lax.rem(s + d, ns), c) for d in range(1, ns)] + [sibling]
    for p in partners:
        pl.semaphore_signal(barrier, inc=1, device_id=p, device_id_type=MESH)

    loads = [
        pltpu.make_async_copy(src, dst, load_sem.at[k])
        for k, (src, dst) in enumerate(
            ((cot_hbm.at[0], cot), (pre_hbm.at[0], pre), (layer_hbm.at[0], layer.at[1]), (w2_hbm, w2), (w1_hbm, w1))
        )
    ]
    for copy in loads:
        copy.start()

    loads[0].wait()
    for z in range(nz):
        got_cot[mine, z * ny:(z + 1) * ny] = cot[z]
    pl.semaphore_wait(barrier, len(partners))

    def lanes(j, ends):
        start = ends[j - 1] if j else 0
        return pl.ds(start * ny, (ends[j] - start) * ny)

    def start_gather(buf, row, j, ends):
        span = lanes(j, ends)
        sends = []
        for k, d in enumerate(CHIPS):
            copy = pltpu.make_async_remote_copy(
                buf.at[mine, span], buf.at[mine, span], gs.at[row, j, k], gr.at[row, j, k],
                device_id=(s, chip(*d)), device_id_type=MESH,
            )
            copy.start()
            sends.append(copy)
        return sends

    def forward_gather(buf, row, j, ends, sends):
        span = lanes(j, ends)
        passed = []
        for g in GROUPS:
            for k, (dz, _) in enumerate(CHIPS):
                if (dz + g) % levels == 0:
                    sends[k].wait_recv()
            block = pl.ds(pl.multiple_of(core * half + lax.rem(zc + g, levels) * (2 * own), own), 2 * own)
            copy = pltpu.make_async_remote_copy(
                buf.at[block, span], buf.at[block, span], fs.at[row, j, g], fr.at[row, j, g],
                device_id=sibling, device_id_type=MESH,
            )
            copy.start()
            passed.append(copy)
        return passed, sends

    def permuted(weight, ordered):
        source = lax.broadcasted_iota(jnp.int32, (2 * half, 2 * half), 0)
        lane = lax.broadcasted_iota(jnp.int32, (1, 2 * half), 1)
        parity = jnp.where(lane < half, 0, 1)
        inner = lane - parity * half
        target = lax.div(inner, own) * (2 * own) + parity * own + lax.rem(inner, own)
        pick = jnp.where(source == target, 1.0, 0.0).astype(jnp.bfloat16)
        ordered[...] = jnp.dot(
            weight[...].reshape(taps * own, 2 * half), pick, preferred_element_type=jnp.float32
        ).astype(jnp.bfloat16)

    def halo(src, dst, sem, there):
        return pltpu.make_async_remote_copy(
            src, dst, hs.at[sem], hr.at[sem], device_id=(there, c), device_id_type=MESH
        )

    up, down = lax.rem(s + 1, ns), lax.rem(s + ns - 1, ns)

    def start_pair(pair):
        @pl.when(s < ns - 1)
        def _():
            pair[0].start()

        @pl.when(s > 0)
        def _():
            pair[1].start()

    def finish_pair(pair, low, high):
        @pl.when(s > 0)
        def _():
            pair[0].wait_recv()

        @pl.when(s == 0)
        def _():
            low[...] = jnp.zeros(low.shape, low.dtype)

        @pl.when(s < ns - 1)
        def _():
            pair[1].wait_recv()

        @pl.when(s == ns - 1)
        def _():
            high[...] = jnp.zeros(high.shape, high.dtype)

    def sent_pair(pair):
        @pl.when(s < ns - 1)
        def _():
            pair[0].wait_send()

        @pl.when(s > 0)
        def _():
            pair[1].wait_send()

    def fill(cols, field, a):
        plane = field[a + 1].astype(jnp.float32).reshape(rows, ny)
        for b in OFFSETS:
            side = moved(plane, b).astype(jnp.bfloat16)
            for e in OFFSETS:
                k = tap(a, b, e)
                for z in range(nz):
                    if 0 <= z + e < nz:
                        piece = side[(z + e) * own:(z + e + 1) * own]
                    else:
                        piece = jnp.zeros((own, ny), jnp.bfloat16)
                    cols[k * own:(k + 1) * own, z * ny:(z + 1) * ny] = piece

    def plane_sum(a, first, last):
        for z in range(first, last):
            total = None
            for b in OFFSETS:
                column = None
                for e in OFFSETS:
                    if 0 <= z - e < nz:
                        k = tap(a, b, e)
                        term = prod[k * own:(k + 1) * own, (z - e) * ny:(z - e + 1) * ny]
                        column = term if column is None else column + term
                column = moved(column, -b)
                total = column if total is None else total + column
            yield z, total

    def input_side(weight, got, row, j, ends_in, ends_out):
        span = lanes(j, ends_in)
        first, last = (ends_out[j - 1] if j else 0), ends_out[j]
        field = got[:, span]

        def product(a):
            lo = tap(a, -1, -1) * own
            left = weight[lo:lo + 9 * own, :]
            prod[lo:lo + 9 * own, span] = jnp.dot(left, field, preferred_element_type=jnp.float32)

        def copy(slot, there):
            part_z = pl.ds(first, last - first)
            return pltpu.make_async_remote_copy(
                send_q.at[row, slot, part_z], recv_q.at[row, slot, part_z], qs.at[row, j, slot], qr.at[row, j, slot],
                device_id=(there, c), device_id_type=MESH,
            )

        pair = copy(0, up), copy(1, down)
        for slot, a in ((0, 1), (1, -1)):
            product(a)
            for z, value in plane_sum(a, first, last):
                send_q[row, slot, z] = value.astype(jnp.bfloat16)

            @pl.when((s < ns - 1) if slot == 0 else (s > 0))
            def _():
                pair[slot].start()
        product(0)
        for z, value in plane_sum(0, first, last):
            center[z * own:(z + 1) * own, :] = value
        return pair

    def input_total(pair, row, j, ends):
        first, last = (ends[j - 1] if j else 0), ends[j]
        part_z = pl.ds(first, last - first)
        finish_pair(pair, recv_q.at[row, 0, part_z], recv_q.at[row, 1, part_z])
        low = recv_q[row, 0, first:last].astype(jnp.float32).reshape((last - first) * own, ny)
        high = recv_q[row, 1, first:last].astype(jnp.float32).reshape((last - first) * own, ny)
        return first, last, center[first * own:last * own, :] + low + high

    def weight_product(cols, got, span):
        value = lax.dot_general(
            got[:, span], cols[:, span], (((1,), (1,)), ((), ())), preferred_element_type=jnp.float32
        )
        return value.reshape(part.shape)

    def block_of(index):
        return pl.ds(pl.multiple_of(index * own, own), own)

    def weight_half(parity, span, add):
        strip = pl.ds(pl.multiple_of(parity * half, half), half)
        piece = lax.dot_general(
            got_pre[strip, span], cols_one[:, span], (((1,), (1,)), ((), ())), preferred_element_type=jnp.float32
        )
        part[parity] = part[parity] + piece if add else piece

    def half_send(turn, parity):
        send_part[1, parity] = part[parity].astype(jnp.bfloat16)
        copies = []
        for d in DISTANCES:
            there = lax.rem(s + d, ns)
            copy = pltpu.make_async_remote_copy(
                send_part.at[1, parity, block_of(there)], recv_part.at[d - 1, parity],
                ws.at[turn, d - 1], wr.at[turn, d - 1], device_id=(there, c), device_id_type=MESH,
            )
            copy.start()
            copies.append(copy)
        return copies

    side = lax.div(s, line)

    def near_send():
        copies = []
        for d in (2, 1, 3):
            place = lax.rem(s + d, line)
            for e in range(2):
                block = block_of(e * line + place)
                copies.append(pltpu.make_async_remote_copy(
                    send_part.at[0, :, block], near.at[d - 1, e], ns_sem.at[d - 1, e], nr_sem.at[d - 1, e],
                    device_id=(side * line + place, c), device_id_type=MESH,
                ))
        for copy in copies:
            copy.start()
        own_parts = [
            part[:, block_of(e * line + lax.rem(s, line)), :] for e in range(2)
        ]
        for e in range(2):
            line_sum[e] = own_parts[e]
        return copies

    def across_send(copies):
        for copy in copies:
            copy.wait_recv()
        for e in range(2):
            total = line_sum[e]
            for d in range(line - 1):
                total = total + near[d, e].astype(jnp.float32)
            line_sum[e] = total
            line_send[e] = total.astype(jnp.bfloat16)
        copy = pltpu.make_async_remote_copy(
            line_send.at[1 - side], opposite, os_sem, or_sem,
            device_id=((1 - side) * line + lax.rem(s, line), c), device_id_type=MESH,
        )
        copy.start()
        return copy

    def across_total(copy, ref):
        copy.wait_recv()
        total = line_sum[side] + opposite[...].astype(jnp.float32)
        ref[...] = (total.reshape(2 * own, -1)[:, :taps * own] * scale).T.reshape(ref.shape)

    def weight_total(copies, ref):
        for copy in copies:
            copy.wait_recv()
        total = part[:, block_of(s), :]
        for d in range(ns - 1):
            total = total + recv_part[d].astype(jnp.float32)
        ref[...] = (total.reshape(2 * own, -1)[:, :taps * own] * scale).T.reshape(ref.shape)

    chunks = len(ends_one)
    started = [start_gather(got_cot, 0, j, ends_one) for j in range(chunks)]

    loads[1].wait()
    value = pre[...].astype(jnp.float32).reshape(rows, ny)
    sig = jax.nn.sigmoid(value)
    hid[1] = (value * sig).astype(jnp.bfloat16).reshape(nz, own, ny)
    slope[...] = sig * (1.0 + value * (1.0 - sig))
    loads[2].wait()
    halo_copies = [
        (halo(hid.at[1], hid.at[0], 0, up), halo(hid.at[1], hid.at[2], 1, down)),
        (halo(layer.at[1], layer.at[0], 2, up), halo(layer.at[1], layer.at[2], 3, down)),
    ]
    for cols in (cols_two, cols_one):
        cols[taps * own:, :] = jnp.zeros((cols.shape[0] - taps * own, nz * ny), jnp.bfloat16)
    fill(cols_two, hid, 0)
    fill(cols_one, layer, 0)
    loads[3].wait()
    permuted(w2, ordered_two)
    loads[4].wait()
    permuted(w1, ordered_one)

    pending, pairs = [], []
    for j in range(chunks):
        passed, sends = forward_gather(got_cot, 0, j, ends_one, started[j])
        for copy in passed:
            copy.wait_recv()
        pending += passed + sends
        pairs.append(input_side(ordered_two, got_cot, 0, j, ends_one, ends_two))
        if j == 0:
            start_pair(halo_copies[0])
    start_pair(halo_copies[1])
    started = []
    for j in range(chunks):
        first, last, grad = input_total(pairs[j], 0, j, ends_two)
        grad = (grad * slope[first * own:last * own, :]).astype(jnp.bfloat16)
        for z in range(first, last):
            got_pre[mine, z * ny:(z + 1) * ny] = grad[(z - first) * own:(z - first + 1) * own]
        started.append(start_gather(got_pre, 1, j, ends_two))
    finish_pair(halo_copies[0], hid.at[0], hid.at[2])
    fill(cols_two, hid, -1)
    fill(cols_two, hid, 1)
    part[...] = weight_product(cols_two, got_cot, pl.ds(0, nz * ny))
    send_part[0] = part[...].astype(jnp.bfloat16)
    near_copies = near_send()

    finish_pair(halo_copies[1], layer.at[0], layer.at[2])
    fill(cols_one, layer, -1)
    fill(cols_one, layer, 1)

    copies_one = []
    for j in range(chunks):
        passed, sends = forward_gather(got_pre, 1, j, ends_two, started[j])
        for turn, parity in enumerate((core, 1 - core)):
            if turn:
                for copy in passed:
                    copy.wait_recv()
            weight_half(parity, lanes(j, ends_two), j > 0)
            if j == chunks - 1:
                copies_one += half_send(turn, parity)
        pending += passed + sends
        if j == chunks - 1:
            across = across_send(near_copies)
        pairs.append(input_side(ordered_one, got_pre, 1, j, ends_two, ends_three))
    for copy in pending + near_copies:
        copy.wait_send()
    for pair in halo_copies + pairs[:chunks]:
        sent_pair(pair)
    for j in range(chunks):
        first, last, grad = input_total(pairs[chunks + j], 1, j, ends_three)
        out_ref[0, first:last] = grad.astype(jnp.bfloat16).reshape(last - first, own, ny)
    across_total(across, two_ref)
    for copy in [across] + copies_one:
        copy.wait_send()
    for pair in pairs[chunks:]:
        sent_pair(pair)
    weight_total(copies_one, one_ref)


def hand_out(one_ref, two_ref, three_ref, one_out, two_out, three_out, sem):
    copies = [
        pltpu.make_async_copy(src, dst, sem.at[k])
        for k, (src, dst) in enumerate(((one_ref, one_out), (two_ref, two_out), (three_ref, three_out)))
    ]
    for copy in copies:
        copy.start()
    for copy in copies:
        copy.wait()


def solution(mesh):
    ns, groups = mesh.shape["space"], mesh.shape["chan"]

    def shards(layer_input, pre_act, out_grad, weight_one, weight_two):
        _, nz, own, ny = layer_input.shape
        taps, _, chans = weight_one.shape
        padded = -(-taps * own // 128) * 128
        scale = float(ns * ny * nz) ** -0.5
        chunks = 2
        ends = tuple(
            tuple(nz if j == chunks - 1 else nz * (j + 1) // chunks + shift for j in range(chunks)) for shift in (1, 0, -1)
        )
        any_space = pl.BlockSpec(memory_space=pl.ANY)
        vmem = pl.BlockSpec(memory_space=pltpu.VMEM)
        bf, f32 = jnp.bfloat16, jnp.float32
        dma = pltpu.SemaphoreType.DMA
        results = pl.pallas_call(
            functools.partial(kernel, (ns, nz, own, ny, scale, ends)),
            out_shape=(
                jax.ShapeDtypeStruct(layer_input.shape, bf),
                jax.ShapeDtypeStruct((taps, own, chans // ns), f32),
                jax.ShapeDtypeStruct((taps, own, chans // ns), f32),
            ),
            in_specs=[any_space] * 5,
            out_specs=(vmem, vmem, vmem),
            scratch_shapes=[
                pltpu.VMEM((3, nz, own, ny), bf),
                pltpu.VMEM((nz, own, ny), bf),
                pltpu.VMEM((nz, own, ny), bf),
                pltpu.VMEM(weight_one.shape, bf),
                pltpu.VMEM(weight_two.shape, bf),
                pltpu.VMEM((taps * own, chans), bf),
                pltpu.VMEM((taps * own, chans), bf),
                pltpu.VMEM((3, nz, own, ny), bf),
                pltpu.VMEM((nz * own, ny), f32),
                pltpu.VMEM((chans, nz * ny), bf),
                pltpu.VMEM((chans, nz * ny), bf),
                pltpu.VMEM((padded, nz * ny), bf),
                pltpu.VMEM((padded, nz * ny), bf),
                pltpu.VMEM((taps * own, nz * ny), f32),
                pltpu.VMEM((nz * own, ny), f32),
                pltpu.VMEM((2, chans // 2, padded), f32),
                pltpu.VMEM((2, 2, chans // 2, padded), bf),
                pltpu.VMEM((ns - 1, 2, own, padded), bf),
                pltpu.VMEM((ns // 2 - 1, 2, 2, own, padded), bf),
                pltpu.VMEM((2, 2, own, padded), f32),
                pltpu.VMEM((2, 2, own, padded), bf),
                pltpu.VMEM((2, own, padded), bf),
                pltpu.VMEM((2, 2, nz, own, ny), bf),
                pltpu.VMEM((2, 2, nz, own, ny), bf),
                dma((5,)),
                dma((2, chunks, len(CHIPS))),
                dma((2, chunks, len(CHIPS))),
                dma((2, chunks, len(GROUPS))),
                dma((2, chunks, len(GROUPS))),
                dma((4,)),
                dma((4,)),
                dma((2, chunks, 2)),
                dma((2, chunks, 2)),
                dma((2, ns - 1)),
                dma((2, ns - 1)),
                dma((ns // 2 - 1, 2)),
                dma((ns // 2 - 1, 2)),
                dma,
                dma,
            ],
            compiler_params=pltpu.CompilerParams(
                collective_id=0, has_side_effects=True, vmem_limit_bytes=48 * 1024 * 1024
            ),
        )(*[pltpu.with_memory_space_constraint(v, pltpu.HBM) for v in (layer_input, pre_act, out_grad, weight_one, weight_two)])
        return pl.pallas_call(
            hand_out,
            out_shape=tuple(jax.ShapeDtypeStruct(v.shape, v.dtype) for v in results),
            in_specs=[vmem] * 3,
            out_specs=(any_space,) * 3,
            scratch_shapes=[dma((3,))],
            compiler_params=pltpu.CompilerParams(vmem_limit_bytes=1024 * 1024),
        )(*results)

    wide, narrow = P("space", None, "chan", None), P(None, "chan", None)
    return jax.shard_map(
        shards,
        mesh=mesh,
        in_specs=(wide, wide, wide, narrow, narrow),
        out_specs=(wide, P(None, "chan", "space"), P(None, "chan", "space")),
        check_vma=False,
    )
```

```python
import functools

import jax
import jax.numpy as jnp
from jax import lax
from jax.experimental import pallas as pl
from jax.experimental.pallas import tpu as pltpu
from jax.sharding import PartitionSpec as P

MESH = pl.DeviceIdType.MESH
OFFSETS = (-1, 0, 1)
CHIPS = ((2, 2), (2, 0), (1, 2), (3, 2), (1, 0), (3, 0), (0, 2))


GROUPS = (3, 1, 0, 2)
DISTANCES = (2, 6, 1, 3, 5, 7, 4)


def tap(a, b, c):
    return 9 * (a + 1) + 3 * (b + 1) + (c + 1)


def moved(value, step):
    if step == 0:
        return value
    width = value.shape[1]
    lane = lax.broadcasted_iota(jnp.int32, value.shape, 1)
    inside = lane < width - step if step > 0 else lane >= -step
    return jnp.where(inside, pltpu.roll(value, (-step) % width, 1), 0.0)


def kernel(
    dims,
    layer_hbm, pre_hbm, cot_hbm, w1_hbm, w2_hbm,
    out_ref, one_ref, two_ref,
    layer, pre, cot, w1, w2, ordered_one, ordered_two, hid, slope,
    got_cot, got_pre, cols_one, cols_two, prod, center,
    part, send_part, recv_part, near, line_sum, line_send, opposite, send_q, recv_q,
    load_sem, gs, gr, fs, fr, hs, hr, qs, qr, ws, wr, ns_sem, nr_sem, os_sem, or_sem,
):
    ns, nz, own, ny, scale, (ends_one, ends_two, ends_three) = dims
    groups = got_cot.shape[0] // own
    rows = own * nz
    line = ns // 2
    taps = w1.shape[0]
    s = lax.axis_index("space")
    c = lax.axis_index("chan")
    zc, wc = lax.div(c, 4), lax.rem(c, 4)
    levels = groups // 4

    def chip(dz, dw):
        return lax.rem(zc + dz, levels) * 4 + (wc ^ dw)

    sibling = (s, c ^ 1)
    core, half = lax.rem(c, 2), got_cot.shape[0] // 2
    mine = pl.ds(pl.multiple_of(core * half + lax.div(c, 2) * own, own), own)

    barrier = pltpu.get_barrier_semaphore()
    partners = [(s, chip(*d)) for d in CHIPS] + [(lax.rem(s + d, ns), c) for d in range(1, ns)] + [sibling]
    for p in partners:
        pl.semaphore_signal(barrier, inc=1, device_id=p, device_id_type=MESH)

    loads = [
        pltpu.make_async_copy(src, dst, load_sem.at[k])
        for k, (src, dst) in enumerate(
            ((cot_hbm.at[0], cot), (pre_hbm.at[0], pre), (layer_hbm.at[0], layer.at[1]), (w2_hbm, w2), (w1_hbm, w1))
        )
    ]
    for copy in loads:
        copy.start()

    loads[0].wait()
    for z in range(nz):
        got_cot[mine, z * ny:(z + 1) * ny] = cot[z]
    pl.semaphore_wait(barrier, len(partners))

    def lanes(j, ends):
        start = ends[j - 1] if j else 0
        return pl.ds(start * ny, (ends[j] - start) * ny)

    def start_gather(buf, row, j, ends):
        span = lanes(j, ends)
        sends = []
        for k, d in enumerate(CHIPS):
            copy = pltpu.make_async_remote_copy(
                buf.at[mine, span], buf.at[mine, span], gs.at[row, j, k], gr.at[row, j, k],
                device_id=(s, chip(*d)), device_id_type=MESH,
            )
            copy.start()
            sends.append(copy)
        return sends

    def forward_gather(buf, row, j, ends, sends):
        span = lanes(j, ends)
        passed = []
        for g in GROUPS:
            for k, (dz, _) in enumerate(CHIPS):
                if (dz + g) % levels == 0:
                    sends[k].wait_recv()
            block = pl.ds(pl.multiple_of(core * half + lax.rem(zc + g, levels) * (2 * own), own), 2 * own)
            copy = pltpu.make_async_remote_copy(
                buf.at[block, span], buf.at[block, span], fs.at[row, j, g], fr.at[row, j, g],
                device_id=sibling, device_id_type=MESH,
            )
            copy.start()
            passed.append(copy)
        return passed, sends

    def permuted(weight, ordered):
        source = lax.broadcasted_iota(jnp.int32, (2 * half, 2 * half), 0)
        lane = lax.broadcasted_iota(jnp.int32, (1, 2 * half), 1)
        parity = jnp.where(lane < half, 0, 1)
        inner = lane - parity * half
        target = lax.div(inner, own) * (2 * own) + parity * own + lax.rem(inner, own)
        pick = jnp.where(source == target, 1.0, 0.0).astype(jnp.bfloat16)
        ordered[...] = jnp.dot(
            weight[...].reshape(taps * own, 2 * half), pick, preferred_element_type=jnp.float32
        ).astype(jnp.bfloat16)

    def halo(src, dst, sem, there):
        return pltpu.make_async_remote_copy(
            src, dst, hs.at[sem], hr.at[sem], device_id=(there, c), device_id_type=MESH
        )

    up, down = lax.rem(s + 1, ns), lax.rem(s + ns - 1, ns)

    def start_pair(pair):
        @pl.when(s < ns - 1)
        def _():
            pair[0].start()

        @pl.when(s > 0)
        def _():
            pair[1].start()

    def finish_pair(pair, low, high):
        @pl.when(s > 0)
        def _():
            pair[0].wait_recv()

        @pl.when(s == 0)
        def _():
            low[...] = jnp.zeros(low.shape, low.dtype)

        @pl.when(s < ns - 1)
        def _():
            pair[1].wait_recv()

        @pl.when(s == ns - 1)
        def _():
            high[...] = jnp.zeros(high.shape, high.dtype)

    def sent_pair(pair):
        @pl.when(s < ns - 1)
        def _():
            pair[0].wait_send()

        @pl.when(s > 0)
        def _():
            pair[1].wait_send()

    def fill(cols, field, a):
        plane = field[a + 1].astype(jnp.float32).reshape(rows, ny)
        for b in OFFSETS:
            side = moved(plane, b).astype(jnp.bfloat16)
            for e in OFFSETS:
                k = tap(a, b, e)
                for z in range(nz):
                    if 0 <= z + e < nz:
                        piece = side[(z + e) * own:(z + e + 1) * own]
                    else:
                        piece = jnp.zeros((own, ny), jnp.bfloat16)
                    cols[k * own:(k + 1) * own, z * ny:(z + 1) * ny] = piece

    def plane_sum(a, first, last):
        for z in range(first, last):
            total = None
            for b in OFFSETS:
                column = None
                for e in OFFSETS:
                    if 0 <= z - e < nz:
                        k = tap(a, b, e)
                        term = prod[k * own:(k + 1) * own, (z - e) * ny:(z - e + 1) * ny]
                        column = term if column is None else column + term
                column = moved(column, -b)
                total = column if total is None else total + column
            yield z, total

    def input_side(weight, got, row, j, ends_in, ends_out):
        span = lanes(j, ends_in)
        first, last = (ends_out[j - 1] if j else 0), ends_out[j]
        field = got[:, span]

        def product(a):
            lo = tap(a, -1, -1) * own
            left = weight[lo:lo + 9 * own, :]
            prod[lo:lo + 9 * own, span] = jnp.dot(left, field, preferred_element_type=jnp.float32)

        def copy(slot, there):
            part_z = pl.ds(first, last - first)
            return pltpu.make_async_remote_copy(
                send_q.at[row, slot, part_z], recv_q.at[row, slot, part_z], qs.at[row, j, slot], qr.at[row, j, slot],
                device_id=(there, c), device_id_type=MESH,
            )

        pair = copy(0, up), copy(1, down)
        for slot, a in ((0, 1), (1, -1)):
            product(a)
            for z, value in plane_sum(a, first, last):
                send_q[row, slot, z] = value.astype(jnp.bfloat16)

            @pl.when((s < ns - 1) if slot == 0 else (s > 0))
            def _():
                pair[slot].start()
        product(0)
        for z, value in plane_sum(0, first, last):
            center[z * own:(z + 1) * own, :] = value
        return pair

    def input_total(pair, row, j, ends):
        first, last = (ends[j - 1] if j else 0), ends[j]
        part_z = pl.ds(first, last - first)
        finish_pair(pair, recv_q.at[row, 0, part_z], recv_q.at[row, 1, part_z])
        low = recv_q[row, 0, first:last].astype(jnp.float32).reshape((last - first) * own, ny)
        high = recv_q[row, 1, first:last].astype(jnp.float32).reshape((last - first) * own, ny)
        return first, last, center[first * own:last * own, :] + low + high

    def weight_product(cols, got, span):
        value = lax.dot_general(
            got[:, span], cols[:, span], (((1,), (1,)), ((), ())), preferred_element_type=jnp.float32
        )
        return value.reshape(part.shape)

    def block_of(index):
        return pl.ds(pl.multiple_of(index * own, own), own)

    def weight_half(parity, span, add):
        strip = pl.ds(pl.multiple_of(parity * half, half), half)
        piece = lax.dot_general(
            got_pre[strip, span], cols_one[:, span], (((1,), (1,)), ((), ())), preferred_element_type=jnp.float32
        )
        part[parity] = part[parity] + piece if add else piece

    def half_send(turn, parity):
        send_part[1, parity] = part[parity].astype(jnp.bfloat16)
        copies = []
        for d in DISTANCES:
            there = lax.rem(s + d, ns)
            copy = pltpu.make_async_remote_copy(
                send_part.at[1, parity, block_of(there)], recv_part.at[d - 1, parity],
                ws.at[turn, d - 1], wr.at[turn, d - 1], device_id=(there, c), device_id_type=MESH,
            )
            copy.start()
            copies.append(copy)
        return copies

    side = lax.div(s, line)

    def near_send():
        copies = []
        for d in (2, 1, 3):
            place = lax.rem(s + d, line)
            for e in range(2):
                block = block_of(e * line + place)
                copies.append(pltpu.make_async_remote_copy(
                    send_part.at[0, :, block], near.at[d - 1, e], ns_sem.at[d - 1, e], nr_sem.at[d - 1, e],
                    device_id=(side * line + place, c), device_id_type=MESH,
                ))
        for copy in copies:
            copy.start()
        own_parts = [
            part[:, block_of(e * line + lax.rem(s, line)), :] for e in range(2)
        ]
        for e in range(2):
            line_sum[e] = own_parts[e]
        return copies

    def across_send(copies):
        for copy in copies:
            copy.wait_recv()
        for e in range(2):
            total = line_sum[e]
            for d in range(line - 1):
                total = total + near[d, e].astype(jnp.float32)
            line_sum[e] = total
            line_send[e] = total.astype(jnp.bfloat16)
        copy = pltpu.make_async_remote_copy(
            line_send.at[1 - side], opposite, os_sem, or_sem,
            device_id=((1 - side) * line + lax.rem(s, line), c), device_id_type=MESH,
        )
        copy.start()
        return copy

    def across_total(copy, ref):
        copy.wait_recv()
        total = line_sum[side] + opposite[...].astype(jnp.float32)
        ref[...] = (total.reshape(2 * own, -1)[:, :taps * own] * scale).T.reshape(ref.shape)

    def weight_total(copies, ref):
        for copy in copies:
            copy.wait_recv()
        total = part[:, block_of(s), :]
        for d in range(ns - 1):
            total = total + recv_part[d].astype(jnp.float32)
        ref[...] = (total.reshape(2 * own, -1)[:, :taps * own] * scale).T.reshape(ref.shape)

    chunks = len(ends_one)
    started = [start_gather(got_cot, 0, j, ends_one) for j in range(chunks)]

    loads[1].wait()
    value = pre[...].astype(jnp.float32).reshape(rows, ny)
    sig = jax.nn.sigmoid(value)
    hid[1] = (value * sig).astype(jnp.bfloat16).reshape(nz, own, ny)
    slope[...] = sig * (1.0 + value * (1.0 - sig))
    loads[2].wait()
    halo_copies = [
        (halo(hid.at[1], hid.at[0], 0, up), halo(hid.at[1], hid.at[2], 1, down)),
        (halo(layer.at[1], layer.at[0], 2, up), halo(layer.at[1], layer.at[2], 3, down)),
    ]
    for cols in (cols_two, cols_one):
        cols[taps * own:, :] = jnp.zeros((cols.shape[0] - taps * own, nz * ny), jnp.bfloat16)
    fill(cols_two, hid, 0)
    fill(cols_one, layer, 0)
    loads[3].wait()
    permuted(w2, ordered_two)
    loads[4].wait()
    permuted(w1, ordered_one)

    pending, pairs = [], []
    for j in range(chunks):
        passed, sends = forward_gather(got_cot, 0, j, ends_one, started[j])
        for copy in passed:
            copy.wait_recv()
        pending += passed + sends
        pairs.append(input_side(ordered_two, got_cot, 0, j, ends_one, ends_two))
        if j == 0:
            start_pair(halo_copies[0])
    start_pair(halo_copies[1])
    started = []
    for j in range(chunks):
        first, last, grad = input_total(pairs[j], 0, j, ends_two)
        grad = (grad * slope[first * own:last * own, :]).astype(jnp.bfloat16)
        for z in range(first, last):
            got_pre[mine, z * ny:(z + 1) * ny] = grad[(z - first) * own:(z - first + 1) * own]
        started.append(start_gather(got_pre, 1, j, ends_two))
    finish_pair(halo_copies[0], hid.at[0], hid.at[2])
    fill(cols_two, hid, -1)
    fill(cols_two, hid, 1)
    part[...] = weight_product(cols_two, got_cot, pl.ds(0, nz * ny))
    send_part[0] = part[...].astype(jnp.bfloat16)
    near_copies = near_send()

    finish_pair(halo_copies[1], layer.at[0], layer.at[2])
    fill(cols_one, layer, -1)
    fill(cols_one, layer, 1)

    copies_one = []
    for j in range(chunks):
        passed, sends = forward_gather(got_pre, 1, j, ends_two, started[j])
        for turn, parity in enumerate((core, 1 - core)):
            if turn:
                for copy in passed:
                    copy.wait_recv()
            weight_half(parity, lanes(j, ends_two), j > 0)
            if j == chunks - 1:
                copies_one += half_send(turn, parity)
        pending += passed + sends
        if j == chunks - 1:
            across = across_send(near_copies)
        pairs.append(input_side(ordered_one, got_pre, 1, j, ends_two, ends_three))
    for copy in pending + near_copies:
        copy.wait_send()
    for pair in halo_copies + pairs[:chunks]:
        sent_pair(pair)
    for j in range(chunks):
        first, last, grad = input_total(pairs[chunks + j], 1, j, ends_three)
        out_ref[0, first:last] = grad.astype(jnp.bfloat16).reshape(last - first, own, ny)
    across_total(across, two_ref)
    for copy in [across] + copies_one:
        copy.wait_send()
    for pair in pairs[chunks:]:
        sent_pair(pair)
    weight_total(copies_one, one_ref)


def hand_out(one_ref, two_ref, three_ref, one_out, two_out, three_out, sem):
    copies = [
        pltpu.make_async_copy(src, dst, sem.at[k])
        for k, (src, dst) in enumerate(((one_ref, one_out), (two_ref, two_out), (three_ref, three_out)))
    ]
    for copy in copies:
        copy.start()
    for copy in copies:
        copy.wait()


def solution(mesh):
    ns, groups = mesh.shape["space"], mesh.shape["chan"]

    def shards(layer_input, pre_act, out_grad, weight_one, weight_two):
        _, nz, own, ny = layer_input.shape
        taps, _, chans = weight_one.shape
        padded = -(-taps * own // 128) * 128
        scale = float(ns * ny * nz) ** -0.5
        chunks = 2
        ends = tuple(
            tuple(nz if j == chunks - 1 else nz * (j + 1) // chunks + shift for j in range(chunks)) for shift in (1, 0, -1)
        )
        any_space = pl.BlockSpec(memory_space=pl.ANY)
        vmem = pl.BlockSpec(memory_space=pltpu.VMEM)
        bf, f32 = jnp.bfloat16, jnp.float32
        dma = pltpu.SemaphoreType.DMA
        results = pl.pallas_call(
            functools.partial(kernel, (ns, nz, own, ny, scale, ends)),
            out_shape=(
                jax.ShapeDtypeStruct(layer_input.shape, bf),
                jax.ShapeDtypeStruct((taps, own, chans // ns), f32),
                jax.ShapeDtypeStruct((taps, own, chans // ns), f32),
            ),
            in_specs=[any_space] * 5,
            out_specs=(vmem, vmem, vmem),
            scratch_shapes=[
                pltpu.VMEM((3, nz, own, ny), bf),
                pltpu.VMEM((nz, own, ny), bf),
                pltpu.VMEM((nz, own, ny), bf),
                pltpu.VMEM(weight_one.shape, bf),
                pltpu.VMEM(weight_two.shape, bf),
                pltpu.VMEM((taps * own, chans), bf),
                pltpu.VMEM((taps * own, chans), bf),
                pltpu.VMEM((3, nz, own, ny), bf),
                pltpu.VMEM((nz * own, ny), f32),
                pltpu.VMEM((chans, nz * ny), bf),
                pltpu.VMEM((chans, nz * ny), bf),
                pltpu.VMEM((padded, nz * ny), bf),
                pltpu.VMEM((padded, nz * ny), bf),
                pltpu.VMEM((taps * own, nz * ny), f32),
                pltpu.VMEM((nz * own, ny), f32),
                pltpu.VMEM((2, chans // 2, padded), f32),
                pltpu.VMEM((2, 2, chans // 2, padded), bf),
                pltpu.VMEM((ns - 1, 2, own, padded), bf),
                pltpu.VMEM((ns // 2 - 1, 2, 2, own, padded), bf),
                pltpu.VMEM((2, 2, own, padded), f32),
                pltpu.VMEM((2, 2, own, padded), bf),
                pltpu.VMEM((2, own, padded), bf),
                pltpu.VMEM((2, 2, nz, own, ny), bf),
                pltpu.VMEM((2, 2, nz, own, ny), bf),
                dma((5,)),
                dma((2, chunks, len(CHIPS))),
                dma((2, chunks, len(CHIPS))),
                dma((2, chunks, len(GROUPS))),
                dma((2, chunks, len(GROUPS))),
                dma((4,)),
                dma((4,)),
                dma((2, chunks, 2)),
                dma((2, chunks, 2)),
                dma((2, ns - 1)),
                dma((2, ns - 1)),
                dma((ns // 2 - 1, 2)),
                dma((ns // 2 - 1, 2)),
                dma,
                dma,
            ],
            compiler_params=pltpu.CompilerParams(
                collective_id=0, has_side_effects=True, vmem_limit_bytes=48 * 1024 * 1024
            ),
        )(*[pltpu.with_memory_space_constraint(v, pltpu.HBM) for v in (layer_input, pre_act, out_grad, weight_one, weight_two)])
        return pl.pallas_call(
            hand_out,
            out_shape=tuple(jax.ShapeDtypeStruct(v.shape, v.dtype) for v in results),
            in_specs=[vmem] * 3,
            out_specs=(any_space,) * 3,
            scratch_shapes=[dma((3,))],
            compiler_params=pltpu.CompilerParams(vmem_limit_bytes=1024 * 1024),
        )(*results)

    wide, narrow = P("space", None, "chan", None), P(None, "chan", None)
    return jax.shard_map(
        shards,
        mesh=mesh,
        in_specs=(wide, wide, wide, narrow, narrow),
        out_specs=(wide, P(None, "chan", "space"), P(None, "chan", "space")),
        check_vma=False,
    )
```
